256 devices in a mesh: coil: 8 (over x, core), slab: 32 (over z, y).
Axes of the slice: x: 4, y: 4, z: 8, core: 2. Of those that a mesh axis runs over, the one named last changes fastest.
Arguments:
- cotangent: float32 [2, 8, 256, 256], P(None, None, 'slab'), may hold values from -40 to 40
- sensitivity: float32 [8, 2, 8, 256, 256], P('coil', None, None, 'slab'), may hold values from -1.5 to 1.5
- kernel: float32 [512, 16, 512], P('slab'), may hold values from 0.2 to 2
- reg_weight: float32 [1], replicated, may hold values from 0.2 to 2
Outputs:
- solution: float32 [2, 8, 256, 256], P(None, None, 'slab')
The draws below stay inside these ranges and needn't reach their ends.
All inputs are finite; a program needn't handle non-finite values.
Results may differ from the reference program's by a relative error of at most 0.0001.
Values sent between devices are 32-bit elements; how exact they have to be, the bound alone decides.
No kernel may reach another device: no remote copies, remote signals or barrier semaphores. Data moves between devices by JAX's collectives and lax.ppermute only.
A program may use at most 64 MiB of HBM per device.

```python
import math
import jax
import jax.numpy as jnp
from jax import lax

IMG = 256
GRID = 512
PLANES = 8
ZGRID = 16
COILS = 8
ITERS = 2


def draw_cotangent(key, part):
    key = jax.random.fold_in(key, 7)
    key_base, key_rows, key_cols = jax.random.split(key, 3)
    base_vals = jnp.clip(jax.random.normal(key_base, (2, PLANES, IMG, IMG), jnp.float32), -4.0, 4.0)
    top_log = math.log(10.0)
    divisor = 10.0
    row_scale = jnp.exp(jax.random.uniform(key_rows, (IMG,), jnp.float32, 0.0, top_log))
    col_scale = jnp.exp(jax.random.uniform(key_cols, (IMG,), jnp.float32, 0.0, top_log))
    return base_vals * row_scale[:, None] * col_scale[None, :] / divisor


def block_scale(key, shape, cuts, smallest, largest):
    factor_of, own = 1.0, jax.random.fold_in(key, 6)
    for axis_at, shards_of in cuts:
        steps = jnp.exp(jax.random.uniform(jax.random.fold_in(own, axis_at), (shards_of,), jnp.float32, smallest / len(cuts), largest / len(cuts)))
        factor_of = factor_of * jnp.repeat(steps, shape[axis_at] // shards_of).reshape([-1 if axis == axis_at else 1 for axis in range(len(shape))])
    return factor_of


def centred(stream_key, extent, spread, bound, pieces=(), held_as=jnp.bfloat16):
    drawn = spread * jax.random.normal(stream_key, extent, jnp.float32)
    if pieces:
        drawn = drawn * block_scale(stream_key, extent, pieces, -0.22, 0.18)
    return jnp.clip(drawn, -bound, bound).astype(held_as)


def setup_inputs(seed: int = 0) -> dict:
    splits = jax.random.split(jax.random.key(seed), 5)
    cotangent = draw_cotangent(jax.random.fold_in(splits[4], 71), 0)
    sensitivity = centred(splits[1], (COILS, 2, PLANES, IMG, IMG), (2 * COILS) ** -0.5, 1.5, ((0, 8), (3, 32)), jnp.float32)
    kernel = jnp.clip(0.2 + 1.8 * jax.random.uniform(splits[2], (GRID, ZGRID, GRID), jnp.float32) ** block_scale(splits[2], (GRID, ZGRID, GRID), ((0, 32),), -0.2, 0.2), 0.2, 2.0)
    reg_weight = jnp.clip(jnp.exp(jax.random.uniform(splits[3], (1,), jnp.float32, math.log(0.2), math.log(2.0))), 0.2, 2.0)
    return {"cotangent": cotangent, "sensitivity": sensitivity, "kernel": kernel, "reg_weight": reg_weight}


def normal_map(vector, sensitivity, kernel, lam_value):
    plane_count = vector.shape[1]
    img_width = vector.shape[-1]
    offset = img_width // 2
    zoff = plane_count // 2
    image_c = vector[0] + 1j * vector[1]
    kernel_t = jnp.transpose(kernel, (1, 2, 0))

    def one_coil(running, coil_sens):
        coil_c = coil_sens[0] + 1j * coil_sens[1]
        padded = jnp.pad(coil_c * image_c, ((zoff, zoff), (offset, offset), (offset, offset)))
        spectrum = jnp.fft.fftn(padded, axes=(0, 1, 2), norm="ortho") * kernel_t
        back_map = jnp.fft.ifftn(spectrum, axes=(0, 1, 2), norm="ortho")
        back_map = back_map[zoff:zoff + plane_count, offset:offset + img_width, offset:offset + img_width]
        return running + jnp.conj(coil_c) * back_map, None

    running, unused = lax.scan(one_coil, jnp.zeros_like(image_c), sensitivity)
    result_c = running + lam_value * image_c
    return jnp.stack([jnp.real(result_c), jnp.imag(result_c)])


def reference(cotangent, sensitivity, kernel, reg_weight):
    lam_value = reg_weight[0]
    solution = jnp.zeros_like(cotangent)
    residual = cotangent
    direction = cotangent
    norm_now = jnp.sum(residual * residual)
    for iteration in range(ITERS):
        image_new = normal_map(direction, sensitivity, kernel, lam_value)
        step_size = norm_now / jnp.sum(direction * image_new)
        solution = solution + step_size * direction
        residual = residual - step_size * image_new
        norm_next = jnp.sum(residual * residual)
        direction = residual + (norm_next / norm_now) * direction
        norm_now = norm_next
    return solution
```

```python
from functools import partial
import math

import jax
import jax.numpy as jnp
import numpy as np
from jax import lax
from jax.experimental import pallas as pl
from jax.experimental.pallas import tpu as pltpu
from jax.sharding import PartitionSpec as P

F32 = jnp.float32
BF16 = jnp.bfloat16
NN = ((1,), (0,))
NT = ((1,), (1,))


def dft(length):
    grid_size = 2 * length
    winding = np.outer(np.arange(length) + length // 2, np.arange(grid_size)) % grid_size
    return np.exp(-2j * np.pi * winding / grid_size) / math.sqrt(grid_size)


def halves(table):
    high = table.astype(np.float32).astype(jnp.bfloat16)
    low = (table - high.astype(np.float64)).astype(np.float32).astype(jnp.bfloat16)
    return high, low


def plane_table(length):
    table = dft(length)
    return np.concatenate([table.real, table.imag], axis=1)


def depth_table(planes, cols):
    table = dft(planes)
    eye = np.eye(cols)
    real = np.einsum("zs,vw->vszw", table.real, eye).reshape(cols * 2 * planes, planes * cols)
    imag = np.einsum("zs,vw->vszw", table.imag, eye).reshape(cols * 2 * planes, planes * cols)
    return np.block([[real, -imag], [imag, real]])


def split(values):
    high = values.astype(BF16)
    low = (values - high.astype(F32)).astype(BF16)
    return high, low


def product(left, right, dims):
    dot = partial(lax.dot_general, dimension_numbers=(dims, ((), ())), preferred_element_type=F32)
    return dot(left[0], right[0]) + (dot(left[1], right[0]) + dot(left[0], right[1]))


def exchange(tiles):
    count = len(tiles)
    width = tiles[0].shape[1]
    step = width // count
    lane = lax.broadcasted_iota(jnp.int32, tiles[0].shape, 1)
    half = 1
    while half < count:
        keep = (lane // (step * half)) % 2 == 0
        out = list(tiles)
        for low in range(count):
            if low & half == 0:
                first, second = tiles[low], tiles[low + half]
                out[low] = jnp.where(keep, first, pltpu.roll(second, step * half, 1))
                out[low + half] = jnp.where(keep, pltpu.roll(first, width - step * half, 1), second)
        tiles = out
        half *= 2
    return tiles


def coil_product(sens_ref, real, imag):
    rows = real.shape[0]
    sens_re, sens_im = sens_ref[:rows], sens_ref[rows:]
    return sens_re * real - sens_im * imag, sens_re * imag + sens_im * real


def send_columns(real, imag, table, out_ref):
    cells = real.shape[0]
    grid_size = 2 * real.shape[1]
    both = product(split(jnp.concatenate([real, imag], axis=0)), table, NN)
    spec = (
        both[:cells, :grid_size] - both[cells:, grid_size:],
        both[:cells, grid_size:] + both[cells:, :grid_size],
    )
    planes, rows, blocks = cells // 8, 8, grid_size // 128
    tiles = [
        jnp.concatenate(
            [
                part[plane * rows : (plane + 1) * rows, block * 128 : (block + 1) * 128]
                for part in spec
                for block in range(blocks)
            ],
            axis=0,
        )
        for plane in range(planes)
    ]
    tiles = exchange(tiles)
    for part in range(2):
        for block in range(blocks):
            for at in range(planes):
                start = (part * blocks + block) * rows
                out_ref[block * planes + at, part * rows : (part + 1) * rows, :] = tiles[at][
                    start : start + rows
                ]


def spectrum(in_ref, table, depth):
    slabs, _, lanes = in_ref.shape
    parts = [in_ref[:, part * 8 : (part + 1) * 8, :].reshape(slabs * 8, lanes) for part in range(2)]
    cells = jnp.concatenate([part.T for part in parts], axis=0)
    grid_size = 2 * slabs * 8
    both = product(split(cells), table, NN)
    spec = jnp.concatenate(
        [
            both[:lanes, :grid_size] - both[lanes:, grid_size:],
            both[:lanes, grid_size:] + both[lanes:, :grid_size],
        ],
        axis=0,
    )
    return product(depth, split(spec), NN)


def total(values):
    return jnp.sum(jnp.sum(values, axis=0, keepdims=True), axis=1, keepdims=True)


def energy(spec, kernel):
    half = kernel.shape[0]
    return total(kernel * (spec[:half] * spec[:half] + spec[half:] * spec[half:]))


def row_of(value, lanes):
    return jnp.broadcast_to(value, (1, lanes))


def start_kernel(vec_ref, sens_ref, high_ref, low_ref, out_ref):
    cells = vec_ref.shape[0] // 2
    real, imag = coil_product(sens_ref, vec_ref[:cells], vec_ref[cells:])
    send_columns(real, imag, (high_ref[...], low_ref[...]), out_ref)


def filter_kernel(
    in_ref, vec_ref, kernel_ref, high_ref, low_ref, deep_high_ref, deep_low_ref, up_high_ref, up_low_ref, out_ref
):
    slabs, _, lanes = in_ref.shape
    high, low = high_ref[...], low_ref[...]
    spec = spectrum(in_ref, (high, low), (deep_high_ref[...], deep_low_ref[...]))
    kernel = kernel_ref[...]
    curvature = energy(spec, kernel)
    half = kernel.shape[0]
    filtered = jnp.concatenate([kernel * spec[:half], kernel * spec[half:]], axis=0)
    shallow = split(product((up_high_ref[...], up_low_ref[...]), split(filtered), NN))
    grid_size = 2 * slabs * 8
    real = product((high[:, :grid_size], low[:, :grid_size]), shallow, NT)
    imag = product((high[:, grid_size:], low[:, grid_size:]), shallow, NT)
    out_ref[:, 0:8, :] = (real[:, :lanes] + imag[:, lanes:]).reshape(slabs, 8, lanes)
    out_ref[:, 8:16, :] = (real[:, lanes:] - imag[:, :lanes]).reshape(slabs, 8, lanes)
    vec = vec_ref[...]
    first = lax.broadcasted_iota(jnp.int32, (8, lanes), 0) == 0
    sums = jnp.where(first, row_of(curvature, lanes), row_of(total(vec * vec), lanes))
    out_ref[:, 16:24, :] = jnp.broadcast_to(sums[None], (slabs, 8, lanes))


def image_kernel(in_ref, sens_ref, high_ref, low_ref, out_ref):
    slabs, _, lanes = in_ref.shape
    planes, blocks = 8, slabs // 8
    tiles = [
        jnp.concatenate(
            [
                in_ref[block * planes + at, part * 8 : (part + 1) * 8, :]
                for part in range(2)
                for block in range(blocks)
            ],
            axis=0,
        )
        for at in range(planes)
    ]
    tiles = exchange(tiles)
    spec = jnp.concatenate(
        [
            jnp.concatenate(
                [
                    tiles[plane][(part * blocks + block) * 8 : (part * blocks + block + 1) * 8]
                    for block in range(blocks)
                ],
                axis=1,
            )
            for part in range(2)
            for plane in range(planes)
        ],
        axis=0,
    )
    spec = split(spec)
    grid_size = blocks * 128
    high, low = high_ref[...], low_ref[...]
    by_real = product(spec, (high[:, :grid_size], low[:, :grid_size]), NT)
    by_imag = product(spec, (high[:, grid_size:], low[:, grid_size:]), NT)
    cells = planes * 8
    img_re = by_real[:cells] + by_imag[cells:]
    img_im = by_real[cells:] - by_imag[:cells]
    sens_re, sens_im = sens_ref[:cells], sens_ref[cells:]
    out_ref[:cells] = sens_re * img_re + sens_im * img_im
    out_ref[cells : 2 * cells] = sens_re * img_im - sens_im * img_re
    sums = jnp.sum(in_ref[:, 16:24, :], axis=0)
    out_ref[2 * cells :] = jnp.concatenate([sums, sums], axis=1)


def add_kernel(own_ref, next_ref, across_ref, last_ref, out_ref):
    out_ref[...] = (own_ref[...] + across_ref[...]) + (next_ref[...] + last_ref[...])


def residual_kernel(
    lam_ref, one_ref, other_ref, vec_ref, sens_ref, high_ref, low_ref, out_ref, res_ref, sums_ref
):
    cells2, width = vec_ref.shape
    cells = cells2 // 2
    lam = lam_ref[0]
    summed = one_ref[...] + other_ref[...]
    vec = vec_ref[...]
    norm = summed[cells2 + 1 : cells2 + 2] * 0.125
    curvature = summed[cells2 : cells2 + 1] + lam * norm
    step = norm / curvature
    image = summed[:cells2] + lam * vec
    residual = vec - step * image
    res_ref[...] = residual
    real, imag = coil_product(sens_ref, residual[:cells], residual[cells:])
    send_columns(real, imag, (high_ref[...], low_ref[...]), out_ref)
    fresh = row_of(total(residual * residual), width)
    cross = row_of(total(residual * image), width)
    row = lax.broadcasted_iota(jnp.int32, (8, width), 0)
    sums_ref[...] = jnp.where(
        row == 0,
        norm,
        jnp.where(row == 1, curvature, jnp.where(row == 2, fresh, cross)),
    )


def last_kernel(in_ref, sums_ref, kernel_ref, high_ref, low_ref, deep_high_ref, deep_low_ref, out_ref):
    table = (high_ref[...], low_ref[...])
    spec = spectrum(in_ref, table, (deep_high_ref[...], deep_low_ref[...]))
    curvature = energy(spec, kernel_ref[...])
    lane = lax.broadcasted_iota(jnp.int32, (1, out_ref.shape[1]), 1)
    lanes = out_ref.shape[1]
    values = jnp.where(
        lane == 0,
        row_of(curvature, lanes),
        jnp.where(lane == 1, sums_ref[2:3, :lanes], sums_ref[3:4, :lanes]),
    )
    out_ref[...] = jnp.broadcast_to(values, out_ref.shape)


def solution_kernel(lam_ref, all_ref, sums_ref, vec_ref, res_ref, out_ref):
    width = vec_ref.shape[1]
    lam = lam_ref[0]
    sums = jnp.sum(all_ref[...], axis=0, keepdims=True)
    lane = lax.broadcasted_iota(jnp.int32, sums.shape, 1)

    def pick(at):
        return row_of(jnp.sum(jnp.where(lane == at, sums, 0.0), axis=1, keepdims=True), width)

    energy_now, fresh, cross = pick(0), pick(1) * 0.125, pick(2) * 0.125
    norm, curvature = sums_ref[0:1], sums_ref[1:2]
    step = norm / curvature
    ratio = fresh / norm
    bent = energy_now + lam * fresh + ratio * (2.0 * cross + ratio * curvature)
    vec = vec_ref[...]
    direction = res_ref[...] + ratio * vec
    out_ref[...] = step * vec + (fresh / bent) * direction


def call(kernel, shapes, scalars=0, inputs=0, limit=16):
    specs = [pl.BlockSpec(memory_space=pltpu.SMEM)] * scalars
    specs += [pl.BlockSpec(memory_space=pltpu.VMEM)] * inputs
    outs = [jax.ShapeDtypeStruct(shape, F32) for shape in shapes]
    places = [pl.BlockSpec(memory_space=pltpu.VMEM)] * len(shapes)
    return pl.pallas_call(
        kernel,
        out_shape=outs if len(outs) > 1 else outs[0],
        in_specs=specs,
        out_specs=places if len(outs) > 1 else places[0],
        compiler_params=pltpu.CompilerParams(vmem_limit_bytes=limit * 2**20),
    )


def shards(cotangent, sensitivity, kernel, reg_weight):
    planes, rows, width = cotangent.shape[1:]
    slabs = lax.axis_size("slab")
    coils = lax.axis_size("coil")
    cols = kernel.shape[0]
    cells2 = 2 * planes * rows
    vec = cotangent.reshape(cells2, width)
    sens = sensitivity.reshape(cells2, width)
    filt = kernel.reshape(cols * kernel.shape[1], kernel.shape[2])
    table = [jnp.asarray(part) for part in halves(plane_table(width))]
    deep = depth_table(planes, cols)
    down = [jnp.asarray(part) for part in halves(deep)]
    up = [jnp.asarray(part) for part in halves(np.ascontiguousarray(deep.T))]
    lanes = planes * cols
    block = (slabs, 2 * rows, lanes)
    to_slabs = partial(lax.all_to_all, axis_name="slab", split_axis=0, concat_axis=0, tiled=True)

    sent = call(start_kernel, [block], 0, 4)(vec, sens, *table)
    got = to_slabs(sent)
    back = call(filter_kernel, [(slabs, 2 * rows + 8, lanes)], 0, 9, 32)(got, vec, filt, *table, *down, *up)
    home = to_slabs(back)
    term = call(image_kernel, [(cells2 + 8, width)], 0, 4)(home, sens, *table)

    chips = coils // 2

    def from_chip(shift):
        pairs = [
            (2 * chip + core, 2 * ((chip + shift) % chips) + core) for chip in range(chips) for core in range(2)
        ]
        return lax.ppermute(term, "coil", pairs)

    pair = call(add_kernel, [term.shape], 0, 4)(term, *[from_chip(shift) for shift in range(1, chips)])
    other = lax.ppermute(pair, "coil", [(at, at ^ 1) for at in range(coils)])
    sent, residual, sums = call(residual_kernel, [block, (cells2, width), (8, width)], 1, 6)(
        reg_weight, pair, other, vec, sens, *table
    )
    got = to_slabs(sent)
    mine = call(last_kernel, [(coils * slabs, 128)], 0, 7, 32)(got, sums, filt, *table, *down)
    every = lax.all_to_all(mine, ("coil", "slab"), 0, 0, tiled=True)
    result = call(solution_kernel, [(cells2, width)], 1, 4)(reg_weight, every, sums, vec, residual)
    return result.reshape(cotangent.shape)


def solution(mesh):
    in_specs = (
        P(None, None, "slab", None),
        P("coil", None, None, "slab", None),
        P("slab", None, None),
        P(),
    )
    out_specs = P(None, None, "slab", None)
    return jax.shard_map(shards, mesh=mesh, in_specs=in_specs, out_specs=out_specs, check_vma=False)
```

```python
from functools import partial
import math

import jax
import jax.numpy as jnp
import numpy as np
from jax import lax
from jax.experimental import pallas as pl
from jax.experimental.pallas import tpu as pltpu
from jax.sharding import PartitionSpec as P

F32 = jnp.float32
BF16 = jnp.bfloat16
NN = ((1,), (0,))
NT = ((1,), (1,))


def dft(length):
    grid_size = 2 * length
    winding = np.outer(np.arange(length) + length // 2, np.arange(grid_size)) % grid_size
    return np.exp(-2j * np.pi * winding / grid_size) / math.sqrt(grid_size)


def halves(table, axis):
    high = table.astype(np.float32).astype(jnp.bfloat16)
    low = (table - high.astype(np.float64)).astype(np.float32).astype(jnp.bfloat16)
    return jnp.asarray(np.concatenate([high, low], axis=axis))


def pair_of(ref, axis):
    half = ref.shape[axis] // 2
    return (ref[:half], ref[half:]) if axis == 0 else (ref[:, :half], ref[:, half:])


def plane_table(length):
    table = dft(length)
    return np.concatenate([table.real, table.imag], axis=1)


def depth_table(planes, cols):
    table = dft(planes)
    eye = np.eye(cols)
    real = np.einsum("zs,vw->vszw", table.real, eye).reshape(cols * 2 * planes, planes * cols)
    imag = np.einsum("zs,vw->vszw", table.imag, eye).reshape(cols * 2 * planes, planes * cols)
    return np.block([[real, -imag], [imag, real]])


def split(values):
    high = values.astype(BF16)
    low = (values - high.astype(F32)).astype(BF16)
    return high, low


def product(left, right, dims):
    dot = partial(lax.dot_general, dimension_numbers=(dims, ((), ())), preferred_element_type=F32)
    return dot(left[0], right[0]) + (dot(left[1], right[0]) + dot(left[0], right[1]))


def exchange(tiles):
    count = len(tiles)
    width = tiles[0].shape[1]
    step = width // count
    lane = lax.broadcasted_iota(jnp.int32, tiles[0].shape, 1)
    half = 1
    while half < count:
        keep = (lane // (step * half)) % 2 == 0
        out = list(tiles)
        for low in range(count):
            if low & half == 0:
                first, second = tiles[low], tiles[low + half]
                out[low] = jnp.where(keep, first, pltpu.roll(second, step * half, 1))
                out[low + half] = jnp.where(keep, pltpu.roll(first, width - step * half, 1), second)
        tiles = out
        half *= 2
    return tiles


def coil_product(sens_ref, real, imag):
    rows = real.shape[0]
    sens_re, sens_im = sens_ref[:rows], sens_ref[rows:]
    return sens_re * real - sens_im * imag, sens_re * imag + sens_im * real


def send_columns(real, imag, table, out_ref):
    cells = real.shape[0]
    grid_size = 2 * real.shape[1]
    both = product(split(jnp.concatenate([real, imag], axis=0)), table, NN)
    spec = (
        both[:cells, :grid_size] - both[cells:, grid_size:],
        both[:cells, grid_size:] + both[cells:, :grid_size],
    )
    planes, rows, blocks = cells // 8, 8, grid_size // 128
    tiles = [
        jnp.concatenate(
            [
                part[plane * rows : (plane + 1) * rows, block * 128 : (block + 1) * 128]
                for part in spec
                for block in range(blocks)
            ],
            axis=0,
        )
        for plane in range(planes)
    ]
    tiles = exchange(tiles)
    for part in range(2):
        for block in range(blocks):
            for at in range(planes):
                start = (part * blocks + block) * rows
                out_ref[block * planes + at, part * rows : (part + 1) * rows, :] = tiles[at][
                    start : start + rows
                ]


def spectrum(in_ref, table, depth):
    slabs, _, lanes = in_ref.shape
    parts = [in_ref[:, part * 8 : (part + 1) * 8, :].reshape(slabs * 8, lanes) for part in range(2)]
    cells = jnp.concatenate([part.T for part in parts], axis=0)
    grid_size = 2 * slabs * 8
    both = product(split(cells), table, NN)
    spec = jnp.concatenate(
        [
            both[:lanes, :grid_size] - both[lanes:, grid_size:],
            both[:lanes, grid_size:] + both[lanes:, :grid_size],
        ],
        axis=0,
    )
    return product(depth, split(spec), NN)


def total(values):
    return jnp.sum(jnp.sum(values, axis=0, keepdims=True), axis=1, keepdims=True)


def energy(spec, kernel):
    half = kernel.shape[0]
    return total(kernel * (spec[:half] * spec[:half] + spec[half:] * spec[half:]))


def row_of(value, lanes):
    return jnp.broadcast_to(value, (1, lanes))


def pick(values, at, lanes):
    lane = lax.broadcasted_iota(jnp.int32, values.shape, 1)
    return row_of(jnp.sum(jnp.where(lane == at, values, 0.0), axis=1, keepdims=True), lanes)


def start_kernel(*refs):
    count = (len(refs) - 2) // 2
    sources, out_ref, loaded, sems = refs[:count], refs[count], refs[count + 1 : -1], refs[-1]
    copies = [
        pltpu.make_async_copy(source, target, sems.at[at]) for at, (source, target) in enumerate(zip(sources, loaded))
    ]
    for copy in copies:
        copy.start()
    for copy in copies[:3]:
        copy.wait()
    vec_ref, sens_ref, table_ref = loaded[:3]
    cells = vec_ref.shape[0] // 2
    real, imag = coil_product(sens_ref, vec_ref[:cells], vec_ref[cells:])
    send_columns(real, imag, pair_of(table_ref, 0), out_ref)
    for copy in copies[3:]:
        copy.wait()


def filter_kernel(in_ref, vec_ref, kernel_ref, table_ref, down_ref, up_ref, out_ref):
    slabs, _, lanes = in_ref.shape
    high, low = pair_of(table_ref, 0)
    spec = spectrum(in_ref, (high, low), pair_of(down_ref, 1))
    kernel = kernel_ref[...]
    curvature = energy(spec, kernel)
    half = kernel.shape[0]
    filtered = jnp.concatenate([kernel * spec[:half], kernel * spec[half:]], axis=0)
    shallow = split(product(pair_of(up_ref, 1), split(filtered), NN))
    grid_size = 2 * slabs * 8
    real = product((high[:, :grid_size], low[:, :grid_size]), shallow, NT)
    imag = product((high[:, grid_size:], low[:, grid_size:]), shallow, NT)
    back_re = real[:, :lanes] + imag[:, lanes:]
    back_im = real[:, lanes:] - imag[:, :lanes]
    vec = vec_ref[...]
    first = lax.broadcasted_iota(jnp.int32, (8, lanes), 0) == 0
    sums = jnp.where(first, row_of(curvature, lanes), row_of(total(vec * vec), lanes))
    out_ref[:, 0:8, :] = back_re.reshape(slabs, 8, lanes)
    out_ref[:, 8:16, :] = back_im.reshape(slabs, 8, lanes)
    out_ref[:, 16:24, :] = jnp.broadcast_to(sums[None], (slabs, 8, lanes))


def image_kernel(in_ref, sens_ref, table_ref, out_ref):
    slabs, _, lanes = in_ref.shape
    planes, blocks = 8, slabs // 8
    tiles = [
        jnp.concatenate(
            [
                in_ref[block * planes + at, part * 8 : (part + 1) * 8, :]
                for part in range(2)
                for block in range(blocks)
            ],
            axis=0,
        )
        for at in range(planes)
    ]
    tiles = exchange(tiles)
    spec = jnp.concatenate(
        [
            jnp.concatenate(
                [
                    tiles[plane][(part * blocks + block) * 8 : (part * blocks + block + 1) * 8]
                    for block in range(blocks)
                ],
                axis=1,
            )
            for part in range(2)
            for plane in range(planes)
        ],
        axis=0,
    )
    spec = split(spec)
    grid_size = blocks * 128
    high, low = pair_of(table_ref, 0)
    by_real = product(spec, (high[:, :grid_size], low[:, :grid_size]), NT)
    by_imag = product(spec, (high[:, grid_size:], low[:, grid_size:]), NT)
    cells = planes * 8
    img_re = by_real[:cells] + by_imag[cells:]
    img_im = by_real[cells:] - by_imag[:cells]
    sens_re, sens_im = sens_ref[:cells], sens_ref[cells:]
    out_ref[:cells] = sens_re * img_re + sens_im * img_im
    out_ref[cells : 2 * cells] = sens_re * img_im - sens_im * img_re
    sums = jnp.sum(in_ref[:, 16:24, :], axis=0)
    out_ref[2 * cells :] = jnp.concatenate([sums, sums], axis=1)


def add_kernel(own_ref, next_ref, across_ref, last_ref, out_ref):
    out_ref[...] = (own_ref[...] + across_ref[...]) + (next_ref[...] + last_ref[...])


def residual_kernel(
    lam_ref, one_ref, other_ref, vec_ref, sens_ref, table_ref, out_ref, res_ref, sums_ref
):
    cells2, width = vec_ref.shape
    cells = cells2 // 2
    lam = lam_ref[0]
    summed = one_ref[...] + other_ref[...]
    vec = vec_ref[...]
    norm = summed[cells2 + 1 : cells2 + 2] * 0.125
    curvature = summed[cells2 : cells2 + 1] + lam * norm
    step = norm / curvature
    image = summed[:cells2] + lam * vec
    residual = vec - step * image
    res_ref[...] = residual
    real, imag = coil_product(sens_ref, residual[:cells], residual[cells:])
    send_columns(real, imag, pair_of(table_ref, 0), out_ref)
    fresh = row_of(total(residual * residual), width)
    cross = row_of(total(residual * image), width)
    row = lax.broadcasted_iota(jnp.int32, (8, width), 0)
    sums_ref[...] = jnp.where(
        row == 0,
        norm,
        jnp.where(row == 1, curvature, jnp.where(row == 2, fresh, cross)),
    )


def last_kernel(in_ref, sums_ref, kernel_ref, table_ref, down_ref, out_ref):
    spec = spectrum(in_ref, pair_of(table_ref, 0), pair_of(down_ref, 1))
    curvature = energy(spec, kernel_ref[...])
    lane = lax.broadcasted_iota(jnp.int32, (1, out_ref.shape[1]), 1)
    lanes = out_ref.shape[1]
    values = jnp.where(
        lane == 0,
        row_of(curvature, lanes),
        jnp.where(lane == 1, sums_ref[2:3, :lanes], sums_ref[3:4, :lanes]),
    )
    out_ref[...] = jnp.broadcast_to(values, out_ref.shape)


def solution_kernel(lam_ref, all_ref, sums_ref, vec_ref, res_ref, out_ref):
    width = vec_ref.shape[1]
    lam = lam_ref[0]
    sums = jnp.sum(all_ref[...], axis=0, keepdims=True)
    energy_now = pick(sums, 0, width)
    fresh, cross = pick(sums, 1, width) * 0.125, pick(sums, 2, width) * 0.125
    norm, curvature = sums_ref[0:1], sums_ref[1:2]
    step = norm / curvature
    ratio = fresh / norm
    bent = energy_now + lam * fresh + ratio * (2.0 * cross + ratio * curvature)
    vec = vec_ref[...]
    direction = res_ref[...] + ratio * vec
    out_ref[...] = step * vec + (fresh / bent) * direction


def call(kernel, shapes, places, scratch=(), limit=16):
    spaces = {"s": pltpu.SMEM, "v": pltpu.VMEM, "h": pltpu.HBM}
    outs = [jax.ShapeDtypeStruct(shape, F32) if isinstance(shape, tuple) else shape for shape in shapes]
    out_specs = [pl.BlockSpec(memory_space=pltpu.VMEM)] * len(shapes)
    return pl.pallas_call(
        kernel,
        out_shape=outs if len(outs) > 1 else outs[0],
        in_specs=[pl.BlockSpec(memory_space=spaces[place]) for place in places],
        out_specs=out_specs if len(outs) > 1 else out_specs[0],
        scratch_shapes=list(scratch),
        compiler_params=pltpu.CompilerParams(vmem_limit_bytes=limit * 2**20),
    )


def shards(cotangent, sensitivity, kernel, reg_weight):
    planes, rows, width = cotangent.shape[1:]
    slabs = lax.axis_size("slab")
    coils = lax.axis_size("coil")
    cols = kernel.shape[0]
    cells2 = 2 * planes * rows
    vec = cotangent.reshape(cells2, width)
    sens = sensitivity.reshape(cells2, width)
    filt = kernel.reshape(cols * kernel.shape[1], kernel.shape[2])
    table = halves(plane_table(width), 0)
    deep = depth_table(planes, cols)
    down, up = halves(deep, 1), halves(deep.T, 1)
    lanes = planes * cols
    block = (slabs, 2 * rows, lanes)
    to_slabs = partial(lax.all_to_all, axis_name="slab", split_axis=0, concat_axis=0, tiled=True)
    dma = pltpu.SemaphoreType.DMA

    sources = [pltpu.with_memory_space_constraint(array, pltpu.HBM) for array in (vec, sens, table, filt, down, up)]
    loaded = [pltpu.VMEM(array.shape, array.dtype) for array in sources]
    sent, vec, sens, table, filt, down, up = call(start_kernel, [block, *loaded], "hhhhhh", [dma((len(sources),))])(
        *sources
    )
    got = to_slabs(sent)
    back = call(filter_kernel, [(slabs, 2 * rows + 8, lanes)], "vvvvvv", (), 32)(got, vec, filt, table, down, up)
    home = to_slabs(back)
    term = call(image_kernel, [(cells2 + 8, width)], "vvv")(home, sens, table)

    chips = coils // 2

    def from_chip(shift):
        pairs = [
            (2 * chip + core, 2 * ((chip + shift) % chips) + core) for chip in range(chips) for core in range(2)
        ]
        return lax.ppermute(term, "coil", pairs)

    across = from_chip(2)
    pair = call(add_kernel, [term.shape], "vvvv")(term, from_chip(1), across, from_chip(3))
    other = lax.ppermute(pair, "coil", [(at, at ^ 1) for at in range(coils)])
    sent, residual, sums = call(residual_kernel, [block, (cells2, width), (8, width)], "svvvvv")(
        reg_weight, pair, other, vec, sens, table
    )
    got = to_slabs(sent)
    own = call(last_kernel, [(coils * slabs, 128)], "vvvvv", (), 32)(got, sums, filt, table, down)
    every = lax.all_to_all(own, ("coil", "slab"), 0, 0, tiled=True)
    result = call(solution_kernel, [(cells2, width)], "svvvv")(reg_weight, every, sums, vec, residual)
    return result.reshape(cotangent.shape)


def solution(mesh):
    in_specs = (
        P(None, None, "slab", None),
        P("coil", None, None, "slab", None),
        P("slab", None, None),
        P(),
    )
    out_specs = P(None, None, "slab", None)
    return jax.shard_map(shards, mesh=mesh, in_specs=in_specs, out_specs=out_specs, check_vma=False)
```

```python
from functools import partial
import math

import jax
import jax.numpy as jnp
import numpy as np
from jax import lax
from jax.experimental import pallas as pl
from jax.experimental.pallas import tpu as pltpu
from jax.sharding import PartitionSpec as P

F32 = jnp.float32
BF16 = jnp.bfloat16
NN = ((1,), (0,))
NT = ((1,), (1,))


def dft(length):
    grid_size = 2 * length
    winding = np.outer(np.arange(length) + length // 2, np.arange(grid_size)) % grid_size
    return np.exp(-2j * np.pi * winding / grid_size) / math.sqrt(grid_size)


def halves(table, axis):
    high = table.astype(np.float32).astype(jnp.bfloat16)
    low = (table - high.astype(np.float64)).astype(np.float32).astype(jnp.bfloat16)
    return jnp.asarray(np.concatenate([high, low], axis=axis))


def pair_of(ref, axis):
    half = ref.shape[axis] // 2
    return (ref[:half], ref[half:]) if axis == 0 else (ref[:, :half], ref[:, half:])


def plane_table(length):
    table = dft(length)
    return np.concatenate([table.real, table.imag], axis=1)


def depth_table(planes, cols):
    table = dft(planes)
    eye = np.eye(cols)
    real = np.einsum("zs,vw->vszw", table.real, eye).reshape(cols * 2 * planes, planes * cols)
    imag = np.einsum("zs,vw->vszw", table.imag, eye).reshape(cols * 2 * planes, planes * cols)
    return np.block([[real, -imag], [imag, real]])


def split(values):
    high = values.astype(BF16)
    low = (values - high.astype(F32)).astype(BF16)
    return high, low


def product(left, right, dims):
    dot = partial(lax.dot_general, dimension_numbers=(dims, ((), ())), preferred_element_type=F32)
    return dot(left[0], right[0]) + (dot(left[1], right[0]) + dot(left[0], right[1]))


def exchange(tiles):
    count = len(tiles)
    width = tiles[0].shape[1]
    step = width // count
    lane = lax.broadcasted_iota(jnp.int32, tiles[0].shape, 1)
    half = 1
    while half < count:
        keep = (lane // (step * half)) % 2 == 0
        out = list(tiles)
        for low in range(count):
            if low & half == 0:
                first, second = tiles[low], tiles[low + half]
                out[low] = jnp.where(keep, first, pltpu.roll(second, step * half, 1))
                out[low + half] = jnp.where(keep, pltpu.roll(first, width - step * half, 1), second)
        tiles = out
        half *= 2
    return tiles


def coil_product(sens_ref, real, imag):
    rows = real.shape[0]
    sens_re, sens_im = sens_ref[:rows], sens_ref[rows:]
    return sens_re * real - sens_im * imag, sens_re * imag + sens_im * real


def send_columns(real, imag, table, out_ref):
    cells = real.shape[0]
    grid_size = 2 * real.shape[1]
    both = product(split(jnp.concatenate([real, imag], axis=0)), table, NN)
    spec = (
        both[:cells, :grid_size] - both[cells:, grid_size:],
        both[:cells, grid_size:] + both[cells:, :grid_size],
    )
    planes, rows, blocks = cells // 8, 8, grid_size // 128
    tiles = [
        jnp.concatenate(
            [
                part[plane * rows : (plane + 1) * rows, block * 128 : (block + 1) * 128]
                for part in spec
                for block in range(blocks)
            ],
            axis=0,
        )
        for plane in range(planes)
    ]
    tiles = exchange(tiles)
    for part in range(2):
        for block in range(blocks):
            for at in range(planes):
                start = (part * blocks + block) * rows
                out_ref[block * planes + at, part * rows : (part + 1) * rows, :] = tiles[at][
                    start : start + rows
                ]


def spectrum(in_ref, table, depth):
    slabs, _, lanes = in_ref.shape
    parts = [in_ref[:, part * 8 : (part + 1) * 8, :].reshape(slabs * 8, lanes) for part in range(2)]
    cells = jnp.concatenate([part.T for part in parts], axis=0)
    grid_size = 2 * slabs * 8
    both = product(split(cells), table, NN)
    spec = jnp.concatenate(
        [
            both[:lanes, :grid_size] - both[lanes:, grid_size:],
            both[:lanes, grid_size:] + both[lanes:, :grid_size],
        ],
        axis=0,
    )
    return product(depth, split(spec), NN)


def total(values):
    return jnp.sum(jnp.sum(values, axis=0, keepdims=True), axis=1, keepdims=True)


def energy(one, other, kernel):
    half = kernel.shape[0]
    return total(kernel * (one[:half] * other[:half] + one[half:] * other[half:]))


def along(part, whole):
    return jnp.where(whole > 0.0, part / jnp.where(whole > 0.0, whole, 1.0), 0.0)


def row_of(value, lanes):
    return jnp.broadcast_to(value, (1, lanes))


def start_kernel(*refs):
    count = (len(refs) - 2) // 2
    sources, out_ref, loaded, sems = refs[:count], refs[count], refs[count + 1 : -1], refs[-1]
    copies = [
        pltpu.make_async_copy(source, target, sems.at[at]) for at, (source, target) in enumerate(zip(sources, loaded))
    ]
    for copy in copies:
        copy.start()
    for copy in copies[:3]:
        copy.wait()
    vec_ref, sens_ref, table_ref = loaded[:3]
    cells = vec_ref.shape[0] // 2
    real, imag = coil_product(sens_ref, vec_ref[:cells], vec_ref[cells:])
    send_columns(real, imag, pair_of(table_ref, 0), out_ref)
    for copy in copies[3:]:
        copy.wait()


def filter_kernel(in_ref, kernel_ref, table_ref, down_ref, up_ref, out_ref, spec_ref, energy_ref):
    slabs, _, lanes = in_ref.shape
    high, low = pair_of(table_ref, 0)
    spec = spectrum(in_ref, (high, low), pair_of(down_ref, 1))
    kernel = kernel_ref[...]
    spec_ref[...] = spec
    energy_ref[...] = jnp.broadcast_to(energy(spec, spec, kernel), energy_ref.shape)
    half = kernel.shape[0]
    filtered = jnp.concatenate([kernel * spec[:half], kernel * spec[half:]], axis=0)
    shallow = split(product(pair_of(up_ref, 1), split(filtered), NN))
    grid_size = 2 * slabs * 8
    real = product((high[:, :grid_size], low[:, :grid_size]), shallow, NT)
    imag = product((high[:, grid_size:], low[:, grid_size:]), shallow, NT)
    out_ref[:, 0:8, :] = (real[:, :lanes] + imag[:, lanes:]).reshape(slabs, 8, lanes)
    out_ref[:, 8:16, :] = (real[:, lanes:] - imag[:, :lanes]).reshape(slabs, 8, lanes)


def image_kernel(in_ref, sens_ref, table_ref, out_ref):
    slabs, _, lanes = in_ref.shape
    planes, blocks = 8, slabs // 8
    tiles = [
        jnp.concatenate(
            [
                in_ref[block * planes + at, part * 8 : (part + 1) * 8, :]
                for part in range(2)
                for block in range(blocks)
            ],
            axis=0,
        )
        for at in range(planes)
    ]
    tiles = exchange(tiles)
    spec = jnp.concatenate(
        [
            jnp.concatenate(
                [
                    tiles[plane][(part * blocks + block) * 8 : (part * blocks + block + 1) * 8]
                    for block in range(blocks)
                ],
                axis=1,
            )
            for part in range(2)
            for plane in range(planes)
        ],
        axis=0,
    )
    spec = split(spec)
    grid_size = blocks * 128
    high, low = pair_of(table_ref, 0)
    by_real = product(spec, (high[:, :grid_size], low[:, :grid_size]), NT)
    by_imag = product(spec, (high[:, grid_size:], low[:, grid_size:]), NT)
    cells = planes * 8
    img_re = by_real[:cells] + by_imag[cells:]
    img_im = by_real[cells:] - by_imag[:cells]
    sens_re, sens_im = sens_ref[:cells], sens_ref[cells:]
    out_ref[:cells] = sens_re * img_re + sens_im * img_im
    out_ref[cells:] = sens_re * img_im - sens_im * img_re


def add_kernel(own_ref, next_ref, across_ref, last_ref, out_ref):
    out_ref[...] = (own_ref[...] + across_ref[...]) + (next_ref[...] + last_ref[...])


def turn_kernel(lam_ref, one_ref, other_ref, vec_ref, sens_ref, table_ref, out_ref, image_ref, sums_ref):
    cells2, width = vec_ref.shape
    cells = cells2 // 2
    vec = vec_ref[...]
    image = (one_ref[...] + other_ref[...]) + lam_ref[0] * vec
    image_ref[...] = image
    real, imag = coil_product(sens_ref, image[:cells], image[cells:])
    send_columns(real, imag, pair_of(table_ref, 0), out_ref)
    norm = total(vec * vec)
    ratio = along(total(vec * image), norm)
    rest = image - ratio * vec
    row = lax.broadcasted_iota(jnp.int32, sums_ref.shape, 0)
    lanes = sums_ref.shape[1]
    sums_ref[...] = jnp.where(
        row == 0,
        row_of(norm, lanes),
        jnp.where(row == 1, row_of(ratio, lanes), row_of(total(rest * rest), lanes)),
    )


def last_kernel(in_ref, before_ref, energy_ref, sums_ref, kernel_ref, table_ref, down_ref, out_ref):
    spec = spectrum(in_ref, pair_of(table_ref, 0), pair_of(down_ref, 1))
    before, kernel = before_ref[...], kernel_ref[...]
    norm = energy_ref[0:1, 0:1]
    ratio = along(energy(before, spec, kernel), norm)
    rest = spec - ratio * before
    lanes = out_ref.shape[1]
    values = [
        row_of(norm, lanes),
        row_of(ratio, lanes),
        row_of(energy(rest, rest, kernel), lanes),
        sums_ref[0:1],
        sums_ref[1:2],
        sums_ref[2:3],
    ]
    lane = lax.broadcasted_iota(jnp.int32, (1, lanes), 1)
    line = values[-1]
    for at, value in enumerate(values[:-1]):
        line = jnp.where(lane == at, value, line)
    out_ref[...] = jnp.broadcast_to(line, out_ref.shape)


def solution_kernel(lam_ref, all_ref, vec_ref, image_ref, out_ref):
    lam = lam_ref[0]
    every = all_ref[...]
    lane = lax.broadcasted_iota(jnp.int32, every.shape, 1)

    def column(at):
        return jnp.sum(jnp.where(lane == at, every, 0.0), axis=1, keepdims=True)

    def sum_of(values):
        return jnp.sum(values, axis=0, keepdims=True)

    deep_norm, deep_ratio, deep_rest, norms, ratios, rests = [column(at) for at in range(6)]
    norm = sum_of(norms) * 0.125
    curvature = sum_of(ratios * norms) * 0.125
    step = norm / curvature
    left, deep_left = 1.0 - step * ratios, 1.0 - step * deep_ratio
    fresh = sum_of(left * left * norms + step * step * rests) * 0.125
    cross = sum_of(ratios * norms * left - step * rests) * 0.125
    energy_now = sum_of(deep_left * deep_left * deep_norm + step * step * deep_rest)
    ratio = fresh / norm
    bent = energy_now + lam * fresh + ratio * (2.0 * cross + ratio * curvature)
    step_now = along(fresh, bent)
    vec = vec_ref[...]
    residual = vec - step * image_ref[...]
    out_ref[...] = step * vec + step_now * (residual + ratio * vec)


def call(kernel, shapes, places, scratch=(), limit=16):
    spaces = {"s": pltpu.SMEM, "v": pltpu.VMEM, "h": pltpu.HBM}
    outs = [jax.ShapeDtypeStruct(shape, F32) if isinstance(shape, tuple) else shape for shape in shapes]
    out_specs = [pl.BlockSpec(memory_space=pltpu.VMEM)] * len(shapes)
    return pl.pallas_call(
        kernel,
        out_shape=outs if len(outs) > 1 else outs[0],
        in_specs=[pl.BlockSpec(memory_space=spaces[place]) for place in places],
        out_specs=out_specs if len(outs) > 1 else out_specs[0],
        scratch_shapes=list(scratch),
        compiler_params=pltpu.CompilerParams(vmem_limit_bytes=limit * 2**20),
    )


def shards(cotangent, sensitivity, kernel, reg_weight):
    planes, rows, width = cotangent.shape[1:]
    slabs = lax.axis_size("slab")
    coils = lax.axis_size("coil")
    cols = kernel.shape[0]
    cells2 = 2 * planes * rows
    vec = cotangent.reshape(cells2, width)
    sens = sensitivity.reshape(cells2, width)
    filt = kernel.reshape(cols * kernel.shape[1], kernel.shape[2])
    table = halves(plane_table(width), 0)
    deep = depth_table(planes, cols)
    down, up = halves(deep, 1), halves(deep.T, 1)
    lanes = planes * cols
    block = (slabs, 2 * rows, lanes)
    to_slabs = partial(lax.all_to_all, axis_name="slab", split_axis=0, concat_axis=0, tiled=True)
    dma = pltpu.SemaphoreType.DMA

    sources = [pltpu.with_memory_space_constraint(array, pltpu.HBM) for array in (vec, sens, table, filt, down, up)]
    loaded = [pltpu.VMEM(array.shape, array.dtype) for array in sources]
    sent, vec, sens, table, filt, down, up = call(start_kernel, [block, *loaded], "hhhhhh", [dma((len(sources),))])(
        *sources
    )
    got = to_slabs(sent)
    back, before, energy_now = call(filter_kernel, [block, (deep.shape[0], 2 * width), (8, 128)], "vvvvv", (), 32)(
        got, filt, table, down, up
    )
    home = to_slabs(back)
    term = call(image_kernel, [(cells2, width)], "vvv")(home, sens, table)

    chips = coils // 2

    def from_chip(shift):
        pairs = [
            (2 * chip + core, 2 * ((chip + shift) % chips) + core) for chip in range(chips) for core in range(2)
        ]
        return lax.ppermute(term, "coil", pairs)

    across = from_chip(2)
    pair = call(add_kernel, [term.shape], "vvvv")(term, from_chip(1), across, from_chip(3))
    other = lax.ppermute(pair, "coil", [(at, at ^ 1) for at in range(coils)])
    sent, image, sums = call(turn_kernel, [block, (cells2, width), (8, 128)], "svvvvv")(
        reg_weight, pair, other, vec, sens, table
    )
    got = to_slabs(sent)
    own = call(last_kernel, [(coils * slabs, 128)], "vvvvvvv", (), 32)(
        got, before, energy_now, sums, filt, table, down
    )
    every = lax.all_to_all(own, ("coil", "slab"), 0, 0, tiled=True)
    result = call(solution_kernel, [(cells2, width)], "svvv")(reg_weight, every, vec, image)
    return result.reshape(cotangent.shape)


def solution(mesh):
    in_specs = (
        P(None, None, "slab", None),
        P("coil", None, None, "slab", None),
        P("slab", None, None),
        P(),
    )
    out_specs = P(None, None, "slab", None)
    return jax.shard_map(shards, mesh=mesh, in_specs=in_specs, out_specs=out_specs, check_vma=False)
```

```python
from functools import partial
import math

import jax
import jax.numpy as jnp
import numpy as np
from jax import lax
from jax.experimental import pallas as pl
from jax.experimental.pallas import tpu as pltpu
from jax.sharding import PartitionSpec as P

F32 = jnp.float32
BF16 = jnp.bfloat16
NN = ((1,), (0,))
NT = ((1,), (1,))


def dft(length):
    grid_size = 2 * length
    winding = np.outer(np.arange(length) + length // 2, np.arange(grid_size)) % grid_size
    return np.exp(-2j * np.pi * winding / grid_size) / math.sqrt(grid_size)


def halves(table, axis):
    high = table.astype(np.float32).astype(jnp.bfloat16)
    low = (table - high.astype(np.float64)).astype(np.float32).astype(jnp.bfloat16)
    return jnp.asarray(np.concatenate([high, low], axis=axis))


def pair_of(ref, axis):
    half = ref.shape[axis] // 2
    return (ref[:half], ref[half:]) if axis == 0 else (ref[:, :half], ref[:, half:])


def plane_table(length):
    table = dft(length)
    return np.concatenate([table.real, table.imag], axis=1)


def rows_table(length, slabs, scale):
    pairs = length // slabs // 2
    table = scale * dft(length)[:, :length].reshape(slabs, pairs, 2, length).transpose(2, 0, 1, 3)
    out = np.empty((2, slabs, 2, pairs, 2, length))
    out[:, :, 0, :, 0], out[:, :, 1, :, 0] = table.real, -table.imag
    out[:, :, 0, :, 1], out[:, :, 1, :, 1] = table.imag, table.real
    return out.reshape(2 * length, 2 * length)


def split(values):
    high = values.astype(BF16)
    low = (values - high.astype(F32)).astype(BF16)
    return high, low


def product(left, right, dims):
    dot = partial(lax.dot_general, dimension_numbers=(dims, ((), ())), preferred_element_type=F32)
    return dot(left[0], right[0]) + (dot(left[1], right[0]) + dot(left[0], right[1]))


def exchange(tiles):
    count = len(tiles)
    width = tiles[0].shape[1]
    step = width // count
    lane = lax.broadcasted_iota(jnp.int32, tiles[0].shape, 1)
    half = 1
    while half < count:
        keep = (lane // (step * half)) % 2 == 0
        out = list(tiles)
        for low in range(count):
            if low & half == 0:
                first, second = tiles[low], tiles[low + half]
                out[low] = jnp.where(keep, first, pltpu.roll(second, step * half, 1))
                out[low + half] = jnp.where(keep, pltpu.roll(first, width - step * half, 1), second)
        tiles = out
        half *= 2
    return tiles


def coil_product(sens_ref, real, imag):
    rows = real.shape[0]
    sens_re, sens_im = sens_ref[:rows], sens_ref[rows:]
    return sens_re * real - sens_im * imag, sens_re * imag + sens_im * real


def send_columns(real, imag, table, out_ref, straight_ref, turned_ref):
    cells, width = real.shape
    rows, grid_size = 8, 2 * width
    planes, blocks = cells // rows, grid_size // 128
    for plane in range(planes):
        for lanes in range(0, width, 128):
            at = 2 * rows * plane + lanes // 128 * 2 * cells
            one = real[rows * plane : rows * (plane + 1), lanes : lanes + 128]
            other = imag[rows * plane : rows * (plane + 1), lanes : lanes + 128]
            straight_ref[at : at + rows], straight_ref[at + rows : at + 2 * rows] = one, other
            turned_ref[at : at + rows], turned_ref[at + rows : at + 2 * rows] = -other, one

    def by_parity(ref):
        parts = [
            jnp.concatenate(
                [ref[pl.ds(lanes * 2 * cells + parity, cells, stride=2), :] for lanes in range(width // 128)], axis=1
            )
            for parity in range(2)
        ]
        return split(jnp.concatenate(parts, axis=0))

    high, low = table
    spec = product(by_parity(straight_ref), (high[:, :grid_size], low[:, :grid_size]), NN)
    spec = spec + product(by_parity(turned_ref), (high[:, grid_size:], low[:, grid_size:]), NN)
    tiles = [
        jnp.concatenate(
            [
                spec[(parity * planes + plane) * rows :][:rows, block * 128 : (block + 1) * 128]
                for parity in range(2)
                for block in range(blocks)
            ],
            axis=0,
        )
        for plane in range(planes)
    ]
    tiles = exchange(tiles)
    for parity in range(2):
        for block in range(blocks):
            for at in range(planes):
                start = (parity * blocks + block) * rows
                out_ref[block * planes + at, parity * rows : (parity + 1) * rows, :] = tiles[at][
                    start : start + rows
                ]


def turn(value, power):
    real, imag = value
    power %= 16
    if power == 0:
        return real, imag
    if power == 4:
        return imag, -real
    if power == 8:
        return -real, -imag
    if power == 12:
        return -imag, real
    cos, sin = math.cos(math.pi * power / 8), -math.sin(math.pi * power / 8)
    return cos * real - sin * imag, cos * imag + sin * real


def plus(one, other):
    return one[0] + other[0], one[1] + other[1]


def minus(one, other):
    return one[0] - other[0], one[1] - other[1]


def four(values, power):
    even, even_off = plus(values[0], values[2]), minus(values[0], values[2])
    odd, odd_off = plus(values[1], values[3]), turn(minus(values[1], values[3]), power)
    return plus(even, odd), plus(even_off, odd_off), minus(even, odd), minus(even_off, odd_off)


def deepen(cells):
    out = [None] * 16
    for rest in range(4):
        folded = [plus(cells[at], turn(cells[at + 4], 4 * rest)) for at in range(4)]
        folded = [turn(value, (at + 4) * rest) for at, value in enumerate(folded)]
        for at, value in enumerate(four(folded, 4)):
            out[4 * at + rest] = value
    return out


def shallow(freqs):
    out = [None] * 8
    for rest in range(4):
        folded = four([freqs[4 * at + rest] for at in range(4)], -4)
        for at in range(4):
            value = turn(folded[at], -(at + 4) * rest)
            above = turn(value, -4 * rest)
            out[at] = value if rest == 0 else plus(out[at], value)
            out[at + 4] = above if rest == 0 else plus(out[at + 4], above)
    return out


def spectrum(in_ref, rows_ref):
    slabs, _, lanes = in_ref.shape
    high, low = pair_of(rows_ref, 0)
    length = high.shape[0] // 2
    parity = []
    for at in range(2):
        cells = in_ref[:, at * 8 : (at + 1) * 8, :].reshape(slabs * 8, lanes).T
        rows = slice(at * length, (at + 1) * length)
        parity.append(product(split(cells), (high[rows], low[rows]), NN))
    total_of, differ = parity[0] + parity[1], parity[0] - parity[1]
    real = jnp.concatenate([total_of[:, :length], differ[:, :length]], axis=1)
    imag = jnp.concatenate([total_of[:, length:], differ[:, length:]], axis=1)
    cols = lanes // 8
    return deepen([(real[at * cols : (at + 1) * cols], imag[at * cols : (at + 1) * cols]) for at in range(8)])


def at_depth(ref, at):
    cols = 16
    tiles = [
        ref[pl.ds(tile * 16 * cols + at, cols, stride=16), :] for tile in range(ref.shape[0] // (16 * cols))
    ]
    return jnp.concatenate(tiles, axis=1)


def total(values):
    return jnp.sum(jnp.sum(values, axis=0, keepdims=True), axis=1, keepdims=True)


def along(part, whole):
    return jnp.where(whole > 0.0, part / jnp.where(whole > 0.0, whole, 1.0), 0.0)


def row_of(value, lanes):
    return jnp.broadcast_to(value, (1, lanes))


def start_kernel(*refs):
    count = (len(refs) - 4) // 2
    sources, out_ref, loaded = refs[:count], refs[count], refs[count + 1 : 2 * count + 1]
    sems, *spaces = refs[2 * count + 1 :]
    pairs = []
    for source, target in zip(sources, loaded):
        rows, lanes = source.shape[0], target.shape[1]
        for tile in range(source.shape[1] // lanes):
            pairs.append((source.at[:, pl.ds(tile * lanes, lanes)], target.at[pl.ds(tile * rows, rows)]))
    copies = [pltpu.make_async_copy(*pair, sems.at[at]) for at, pair in enumerate(pairs)]
    for copy in copies:
        copy.start()
    for copy in copies[:3]:
        copy.wait()
    vec_ref, sens_ref, table_ref = loaded[:3]
    cells = vec_ref.shape[0] // 2
    real, imag = coil_product(sens_ref, vec_ref[:cells], vec_ref[cells:])
    send_columns(real, imag, pair_of(table_ref, 0), out_ref, *spaces)
    for copy in copies[3:]:
        copy.wait()


def filter_kernel(in_ref, kernel_ref, rows_ref, out_ref, spec_ref, energy_ref):
    slabs, _, lanes = in_ref.shape
    spec = spectrum(in_ref, rows_ref)
    cols = lanes // 8
    weight = 0.0
    filtered = []
    for at, (real, imag) in enumerate(spec):
        spec_ref[2 * at * cols : (2 * at + 1) * cols] = real
        spec_ref[(2 * at + 1) * cols : (2 * at + 2) * cols] = imag
        kernel = at_depth(kernel_ref, at)
        filtered.append((kernel * real, kernel * imag))
        weight = weight + (filtered[-1][0] * real + filtered[-1][1] * imag)
    energy_ref[...] = jnp.broadcast_to(total(weight), energy_ref.shape)
    planes = shallow(filtered)
    real, imag = [jnp.concatenate([plane[part] for plane in planes], axis=0) for part in range(2)]
    high, low = pair_of(rows_ref, 0)
    length = high.shape[0] // 2
    for at, join in enumerate((jnp.add, jnp.subtract)):
        folded = [join(part[:, :length], part[:, length:]) for part in (real, imag)]
        rows = slice(at * length, (at + 1) * length)
        back = product((high[rows], low[rows]), split(jnp.concatenate(folded, axis=1)), NT)
        out_ref[:, at * 8 : (at + 1) * 8, :] = back.reshape(slabs, 8, lanes)


def image_kernel(in_ref, sens_ref, table_ref, out_ref, straight_ref, turned_ref):
    slabs, _, lanes = in_ref.shape
    planes, blocks = 8, slabs // 8
    tiles = [
        jnp.concatenate(
            [
                in_ref[block * planes + at, part * 8 : (part + 1) * 8, :]
                for part in range(2)
                for block in range(blocks)
            ],
            axis=0,
        )
        for at in range(planes)
    ]
    tiles = exchange(tiles)
    spec = jnp.concatenate(
        [
            jnp.concatenate(
                [
                    tiles[plane][(part * blocks + block) * 8 : (part * blocks + block + 1) * 8]
                    for block in range(blocks)
                ],
                axis=1,
            )
            for part in range(2)
            for plane in range(planes)
        ],
        axis=0,
    )
    spec = split(spec)
    grid_size = blocks * 128
    high, low = pair_of(table_ref, 0)
    by_real = product(spec, (high[:, :grid_size], low[:, :grid_size]), NT)
    by_imag = product(spec, (high[:, grid_size:], low[:, grid_size:]), NT)
    cells = planes * 8
    tiled = range(by_real.shape[1] // 128)
    for parity in range(2):
        part = slice(parity * cells, (parity + 1) * cells)
        for tile in tiled:
            rows, tile_of = pl.ds(tile * 2 * cells + parity, cells, stride=2), slice(tile * 128, tile * 128 + 128)
            straight_ref[rows, :] = by_real[part, tile_of]
            turned_ref[rows, :] = by_imag[part, tile_of]

    def of_part(ref, part):
        columns = []
        for tile in tiled:
            starts = [tile * 2 * cells + 16 * plane + 8 * part for plane in range(planes)]
            columns.append(jnp.concatenate([ref[start : start + 8] for start in starts], axis=0))
        return jnp.concatenate(columns, axis=1)

    img_re = of_part(straight_ref, 0) + of_part(turned_ref, 1)
    img_im = of_part(straight_ref, 1) - of_part(turned_ref, 0)
    sens_re, sens_im = sens_ref[:cells], sens_ref[cells:]
    out_ref[:cells] = sens_re * img_re + sens_im * img_im
    out_ref[cells:] = sens_re * img_im - sens_im * img_re


def add_kernel(own_ref, next_ref, across_ref, last_ref, out_ref):
    out_ref[...] = (own_ref[...] + across_ref[...]) + (next_ref[...] + last_ref[...])


def turn_kernel(
    lam_ref, one_ref, other_ref, vec_ref, sens_ref, table_ref, out_ref, image_ref, sums_ref, straight_ref, turned_ref
):
    cells2, width = vec_ref.shape
    cells = cells2 // 2
    vec = vec_ref[...]
    image = (one_ref[...] + other_ref[...]) + lam_ref[0] * vec
    image_ref[...] = image
    real, imag = coil_product(sens_ref, image[:cells], image[cells:])
    send_columns(real, imag, pair_of(table_ref, 0), out_ref, straight_ref, turned_ref)
    norm = total(vec * vec)
    ratio = along(total(vec * image), norm)
    rest = image - ratio * vec
    row = lax.broadcasted_iota(jnp.int32, sums_ref.shape, 0)
    lanes = sums_ref.shape[1]
    sums_ref[...] = jnp.where(
        row == 0,
        row_of(norm, lanes),
        jnp.where(row == 1, row_of(ratio, lanes), row_of(total(rest * rest), lanes)),
    )


def last_kernel(in_ref, before_ref, energy_ref, sums_ref, kernel_ref, rows_ref, out_ref):
    spec = spectrum(in_ref, rows_ref)
    cols = spec[0][0].shape[0]
    norm = energy_ref[0:1, 0:1]

    def before(at):
        return before_ref[2 * at * cols : (2 * at + 1) * cols], before_ref[(2 * at + 1) * cols : (2 * at + 2) * cols]

    weight = 0.0
    for at, (real, imag) in enumerate(spec):
        real_0, imag_0 = before(at)
        weight = weight + at_depth(kernel_ref, at) * (real * real_0 + imag * imag_0)
    ratio = along(total(weight), norm)
    weight = 0.0
    for at, (real, imag) in enumerate(spec):
        real_0, imag_0 = before(at)
        real, imag = real - ratio * real_0, imag - ratio * imag_0
        weight = weight + at_depth(kernel_ref, at) * (real * real + imag * imag)
    lanes = out_ref.shape[1]
    values = [
        row_of(norm, lanes),
        row_of(ratio, lanes),
        row_of(total(weight), lanes),
        sums_ref[0:1],
        sums_ref[1:2],
        sums_ref[2:3],
    ]
    lane = lax.broadcasted_iota(jnp.int32, (1, lanes), 1)
    line = values[-1]
    for at, value in enumerate(values[:-1]):
        line = jnp.where(lane == at, value, line)
    out_ref[...] = jnp.broadcast_to(line, out_ref.shape)


def solution_kernel(lam_ref, all_ref, vec_ref, image_ref, out_ref):
    lam = lam_ref[0]
    every = all_ref[...]
    lane = lax.broadcasted_iota(jnp.int32, every.shape, 1)

    def column(at):
        return jnp.sum(jnp.where(lane == at, every, 0.0), axis=1, keepdims=True)

    def sum_of(values):
        return jnp.sum(values, axis=0, keepdims=True)

    deep_norm, deep_ratio, deep_rest, norms, ratios, rests = [column(at) for at in range(6)]
    norm = sum_of(norms) * 0.125
    curvature = sum_of(ratios * norms) * 0.125
    step = norm / curvature
    left, deep_left = 1.0 - step * ratios, 1.0 - step * deep_ratio
    fresh = sum_of(left * left * norms + step * step * rests) * 0.125
    cross = sum_of(ratios * norms * left - step * rests) * 0.125
    energy_now = sum_of(deep_left * deep_left * deep_norm + step * step * deep_rest)
    ratio = fresh / norm
    bent = energy_now + lam * fresh + ratio * (2.0 * cross + ratio * curvature)
    step_now = along(fresh, bent)
    vec = vec_ref[...]
    residual = vec - step * image_ref[...]
    out_ref[...] = step * vec + step_now * (residual + ratio * vec)


def call(kernel, shapes, places, scratch=(), limit=16):
    spaces = {"s": pltpu.SMEM, "v": pltpu.VMEM, "h": pltpu.HBM}
    outs = [jax.ShapeDtypeStruct(shape, F32) if isinstance(shape, tuple) else shape for shape in shapes]
    out_specs = [pl.BlockSpec(memory_space=pltpu.VMEM)] * len(shapes)
    return pl.pallas_call(
        kernel,
        out_shape=outs if len(outs) > 1 else outs[0],
        in_specs=[pl.BlockSpec(memory_space=spaces[place]) for place in places],
        out_specs=out_specs if len(outs) > 1 else out_specs[0],
        scratch_shapes=list(scratch),
        compiler_params=pltpu.CompilerParams(vmem_limit_bytes=limit * 2**20),
    )


def shards(cotangent, sensitivity, kernel, reg_weight):
    planes, rows, width = cotangent.shape[1:]
    slabs = lax.axis_size("slab")
    coils = lax.axis_size("coil")
    cols = kernel.shape[0]
    cells2 = 2 * planes * rows
    vec = cotangent.reshape(cells2, width)
    sens = sensitivity.reshape(cells2, width)
    filt = kernel.reshape(cols * kernel.shape[1], kernel.shape[2])
    table = halves(plane_table(width), 0)
    row_table = halves(rows_table(width, slabs, 1.0 / math.sqrt(2 * planes)), 0)
    lanes = planes * cols
    block = (slabs, 2 * rows, lanes)
    to_slabs = partial(lax.all_to_all, axis_name="slab", split_axis=0, concat_axis=0, tiled=True)
    dma = pltpu.SemaphoreType.DMA

    spaces = [pltpu.VMEM((cells2 * width // 128, 128), F32)] * 2
    sources = [pltpu.with_memory_space_constraint(array, pltpu.HBM) for array in (vec, sens, table, filt, row_table)]
    loaded = [pltpu.VMEM(array.shape, array.dtype) for array in sources]
    loaded[3] = pltpu.VMEM((filt.size // 128, 128), F32)
    sent, vec, sens, table, filt, row_table = call(
        start_kernel, [block, *loaded], "hhhhh", [dma((len(sources) + filt.shape[1] // 128 - 1,)), *spaces]
    )(*sources)
    got = to_slabs(sent)
    back, before, energy_now = call(filter_kernel, [block, (4 * lanes, 2 * width), (8, 128)], "vvv", (), 32)(
        got, filt, row_table
    )
    home = to_slabs(back)
    term = call(image_kernel, [(cells2, width)], "vvv", spaces)(home, sens, table)

    chips = coils // 2

    def from_chip(shift):
        pairs = [
            (2 * chip + core, 2 * ((chip + shift) % chips) + core) for chip in range(chips) for core in range(2)
        ]
        return lax.ppermute(term, "coil", pairs)

    across = from_chip(2)
    pair = call(add_kernel, [term.shape], "vvvv")(term, from_chip(1), across, from_chip(3))
    other = lax.ppermute(pair, "coil", [(at, at ^ 1) for at in range(coils)])
    sent, image, sums = call(turn_kernel, [block, (cells2, width), (8, 128)], "svvvvv", spaces)(
        reg_weight, pair, other, vec, sens, table
    )
    got = to_slabs(sent)
    own = call(last_kernel, [(coils * slabs, 128)], "vvvvvv", (), 32)(
        got, before, energy_now, sums, filt, row_table
    )
    every = lax.all_to_all(own, ("coil", "slab"), 0, 0, tiled=True)
    result = call(solution_kernel, [(cells2, width)], "svvv")(reg_weight, every, vec, image)
    return result.reshape(cotangent.shape)


def solution(mesh):
    in_specs = (
        P(None, None, "slab", None),
        P("coil", None, None, "slab", None),
        P("slab", None, None),
        P(),
    )
    out_specs = P(None, None, "slab", None)
    return jax.shard_map(shards, mesh=mesh, in_specs=in_specs, out_specs=out_specs, check_vma=False)
```

```python
from functools import partial
import math

import jax
import jax.numpy as jnp
import numpy as np
from jax import lax
from jax.experimental import pallas as pl
from jax.experimental.pallas import tpu as pltpu
from jax.sharding import PartitionSpec as P

F32 = jnp.float32
BF16 = jnp.bfloat16
NN = ((1,), (0,))
NT = ((1,), (1,))


def dft(length):
    grid_size = 2 * length
    winding = np.outer(np.arange(length) + length // 2, np.arange(grid_size)) % grid_size
    return np.exp(-2j * np.pi * winding / grid_size) / math.sqrt(grid_size)


def halves(table, axis):
    high = table.astype(np.float32).astype(jnp.bfloat16)
    low = (table - high.astype(np.float64)).astype(np.float32).astype(jnp.bfloat16)
    return jnp.asarray(np.concatenate([high, low], axis=axis))


def pair_of(ref, axis):
    half = ref.shape[axis] // 2
    return (ref[:half], ref[half:]) if axis == 0 else (ref[:, :half], ref[:, half:])


def plane_table(length):
    table = dft(length)
    return np.concatenate([table.real, table.imag], axis=1)


def rows_table(length, slabs, scale):
    pairs = length // slabs // 2
    table = scale * dft(length)[:, :length].reshape(slabs, pairs, 2, length).transpose(2, 0, 1, 3)
    out = np.empty((2, slabs, 2, pairs, 2, length))
    out[:, :, 0, :, 0], out[:, :, 1, :, 0] = table.real, -table.imag
    out[:, :, 0, :, 1], out[:, :, 1, :, 1] = table.imag, table.real
    return out.reshape(2 * length, 2 * length)


def split(values):
    high = values.astype(BF16)
    low = (values - high.astype(F32)).astype(BF16)
    return high, low


def product(left, right, dims):
    dot = partial(lax.dot_general, dimension_numbers=(dims, ((), ())), preferred_element_type=F32)
    rows, cols = left[0].shape[0], right[0].shape[1 - dims[1][0]]
    if dims == NT and cols <= 128:
        both = dot(left[0], jnp.concatenate(right, axis=0))
        return (both[:, :cols] + both[:, cols:]) + dot(left[1], right[0])
    both = dot(jnp.concatenate(left, axis=0), right[0])
    return (both[:rows] + both[rows:]) + dot(left[0], right[1])


def exchange(tiles):
    count = len(tiles)
    width = tiles[0].shape[1]
    step = width // count
    group = lax.broadcasted_iota(jnp.int32, tiles[0].shape, 1) // step
    tiles = [pltpu.roll(tile, step * at, 1) if at else tile for at, tile in enumerate(tiles)]
    half = 1
    while half < count:
        later = (group // half) % 2 == 1
        tiles = [jnp.where(later, tiles[(at + half) % count], tiles[at]) for at in range(count)]
        half *= 2
    return [pltpu.roll(tiles[-at], width - step * at, 1) if at else tiles[0] for at in range(count)]


def coil_product(sens_ref, real, imag):
    rows = real.shape[0]
    sens_re, sens_im = sens_ref[:rows], sens_ref[rows:]
    return sens_re * real - sens_im * imag, sens_re * imag + sens_im * real


def send_columns(real, imag, table, out_ref, straight_ref, turned_ref):
    cells, width = real.shape
    rows, grid_size = 8, 2 * width
    planes, blocks = cells // rows, grid_size // 128
    for plane in range(planes):
        for lanes in range(0, width, 128):
            at = 2 * rows * plane + lanes // 128 * 2 * cells
            one = real[rows * plane : rows * (plane + 1), lanes : lanes + 128]
            other = imag[rows * plane : rows * (plane + 1), lanes : lanes + 128]
            straight_ref[at : at + rows], straight_ref[at + rows : at + 2 * rows] = one, other
            turned_ref[at : at + rows], turned_ref[at + rows : at + 2 * rows] = -other, one

    def by_parity(ref):
        parts = [
            jnp.concatenate(
                [ref[pl.ds(lanes * 2 * cells + parity, cells, stride=2), :] for lanes in range(width // 128)], axis=1
            )
            for parity in range(2)
        ]
        return split(jnp.concatenate(parts, axis=0))

    straight, turned = by_parity(straight_ref), by_parity(turned_ref)
    high, low = table()
    spec = product(straight, (high[:, :grid_size], low[:, :grid_size]), NN)
    spec = spec + product(turned, (high[:, grid_size:], low[:, grid_size:]), NN)
    tiles = [
        jnp.concatenate(
            [
                spec[(parity * planes + plane) * rows :][:rows, block * 128 : (block + 1) * 128]
                for parity in range(2)
                for block in range(blocks)
            ],
            axis=0,
        )
        for plane in range(planes)
    ]
    tiles = exchange(tiles)
    for parity in range(2):
        for block in range(blocks):
            for at in range(planes):
                start = (parity * blocks + block) * rows
                out_ref[block * planes + at, parity * rows : (parity + 1) * rows, :] = tiles[at][
                    start : start + rows
                ]


def turn(value, power):
    real, imag = value
    power %= 16
    if power == 0:
        return real, imag
    if power == 4:
        return imag, -real
    if power == 8:
        return -real, -imag
    if power == 12:
        return -imag, real
    cos, sin = math.cos(math.pi * power / 8), -math.sin(math.pi * power / 8)
    return cos * real - sin * imag, cos * imag + sin * real


def plus(one, other):
    return one[0] + other[0], one[1] + other[1]


def minus(one, other):
    return one[0] - other[0], one[1] - other[1]


def four(values, power):
    even, even_off = plus(values[0], values[2]), minus(values[0], values[2])
    odd, odd_off = plus(values[1], values[3]), turn(minus(values[1], values[3]), power)
    return plus(even, odd), plus(even_off, odd_off), minus(even, odd), minus(even_off, odd_off)


def deepen(cells):
    out = [None] * 16
    for rest in range(4):
        folded = [plus(cells[at], turn(cells[at + 4], 4 * rest)) for at in range(4)]
        folded = [turn(value, (at + 4) * rest) for at, value in enumerate(folded)]
        for at, value in enumerate(four(folded, 4)):
            out[4 * at + rest] = value
    return out


def shallow(freqs):
    out = [None] * 8
    for rest in range(4):
        folded = four([freqs[4 * at + rest] for at in range(4)], -4)
        for at in range(4):
            value = turn(folded[at], -(at + 4) * rest)
            above = turn(value, -4 * rest)
            out[at] = value if rest == 0 else plus(out[at], value)
            out[at + 4] = above if rest == 0 else plus(out[at + 4], above)
    return out


def spectrum(in_ref, rows_ref):
    slabs, _, lanes = in_ref.shape
    high, low = pair_of(rows_ref, 0)
    length = high.shape[0] // 2
    parity = []
    for at in range(2):
        cells = in_ref[:, at * 8 : (at + 1) * 8, :].reshape(slabs * 8, lanes).T
        rows = slice(at * length, (at + 1) * length)
        parity.append(product(split(cells), (high[rows], low[rows]), NN))
    total_of, differ = parity[0] + parity[1], parity[0] - parity[1]
    real = jnp.concatenate([total_of[:, :length], differ[:, :length]], axis=1)
    imag = jnp.concatenate([total_of[:, length:], differ[:, length:]], axis=1)
    cols = lanes // 8
    return deepen([(real[at * cols : (at + 1) * cols], imag[at * cols : (at + 1) * cols]) for at in range(8)])


def at_depth(ref, at):
    cols = 16
    tiles = [
        ref[pl.ds(tile * 16 * cols + at, cols, stride=16), :] for tile in range(ref.shape[0] // (16 * cols))
    ]
    return jnp.concatenate(tiles, axis=1)


def total(values):
    return jnp.sum(jnp.sum(values, axis=0, keepdims=True), axis=1, keepdims=True)


def along(part, whole):
    return jnp.where(whole > 0.0, part / jnp.where(whole > 0.0, whole, 1.0), 0.0)


def row_of(value, lanes):
    return jnp.broadcast_to(value, (1, lanes))


def start_kernel(*refs):
    count = (len(refs) - 4) // 2
    sources, out_ref, loaded = refs[:count], refs[count], refs[count + 1 : 2 * count + 1]
    sems, *spaces = refs[2 * count + 1 :]
    pairs = []
    for source, target in zip(sources, loaded):
        rows, lanes = source.shape[0], target.shape[1]
        for tile in range(source.shape[1] // lanes):
            pairs.append((source.at[:, pl.ds(tile * lanes, lanes)], target.at[pl.ds(tile * rows, rows)]))
    copies = [pltpu.make_async_copy(*pair, sems.at[at]) for at, pair in enumerate(pairs)]
    for copy in copies:
        copy.start()
    for copy in copies[:2]:
        copy.wait()
    vec_ref, sens_ref, table_ref = loaded[:3]
    cells = vec_ref.shape[0] // 2
    real, imag = coil_product(sens_ref, vec_ref[:cells], vec_ref[cells:])

    def table():
        copies[2].wait()
        return pair_of(table_ref, 0)

    send_columns(real, imag, table, out_ref, *spaces)
    for copy in copies[3:]:
        copy.wait()


def filter_kernel(in_ref, kernel_ref, rows_ref, out_ref, spec_ref, energy_ref, by_depth_ref):
    slabs, _, lanes = in_ref.shape
    spec = spectrum(in_ref, rows_ref)
    cols = lanes // 8
    weight = 0.0
    filtered = []
    for at, (real, imag) in enumerate(spec):
        spec_ref[2 * at * cols : (2 * at + 1) * cols] = real
        spec_ref[(2 * at + 1) * cols : (2 * at + 2) * cols] = imag
        kernel = at_depth(kernel_ref, at)
        by_depth_ref[at * cols : (at + 1) * cols] = kernel
        filtered.append((kernel * real, kernel * imag))
        weight = weight + (filtered[-1][0] * real + filtered[-1][1] * imag)
    energy_ref[...] = jnp.broadcast_to(total(weight), energy_ref.shape)
    planes = shallow(filtered)
    real, imag = [jnp.concatenate([plane[part] for plane in planes], axis=0) for part in range(2)]
    high, low = pair_of(rows_ref, 0)
    length = high.shape[0] // 2
    for at, join in enumerate((jnp.add, jnp.subtract)):
        folded = [join(part[:, :length], part[:, length:]) for part in (real, imag)]
        rows = slice(at * length, (at + 1) * length)
        back = product((high[rows], low[rows]), split(jnp.concatenate(folded, axis=1)), NT)
        out_ref[:, at * 8 : (at + 1) * 8, :] = back.reshape(slabs, 8, lanes)


def image_kernel(in_ref, sens_ref, table_ref, out_ref, straight_ref, turned_ref):
    slabs, _, lanes = in_ref.shape
    planes, blocks = 8, slabs // 8
    tiles = [
        jnp.concatenate(
            [
                in_ref[block * planes + at, part * 8 : (part + 1) * 8, :]
                for part in range(2)
                for block in range(blocks)
            ],
            axis=0,
        )
        for at in range(planes)
    ]
    tiles = exchange(tiles)
    spec = jnp.concatenate(
        [
            jnp.concatenate(
                [
                    tiles[plane][(part * blocks + block) * 8 : (part * blocks + block + 1) * 8]
                    for block in range(blocks)
                ],
                axis=1,
            )
            for part in range(2)
            for plane in range(planes)
        ],
        axis=0,
    )
    spec = split(spec)
    grid_size = blocks * 128
    high, low = pair_of(table_ref, 0)
    by_real = product(spec, (high[:, :grid_size], low[:, :grid_size]), NT)
    by_imag = product(spec, (high[:, grid_size:], low[:, grid_size:]), NT)
    cells = planes * 8
    tiled = range(by_real.shape[1] // 128)
    for parity in range(2):
        part = slice(parity * cells, (parity + 1) * cells)
        for tile in tiled:
            rows, tile_of = pl.ds(tile * 2 * cells + parity, cells, stride=2), slice(tile * 128, tile * 128 + 128)
            straight_ref[rows, :] = by_real[part, tile_of]
            turned_ref[rows, :] = by_imag[part, tile_of]

    def of_part(ref, part):
        columns = []
        for tile in tiled:
            starts = [tile * 2 * cells + 16 * plane + 8 * part for plane in range(planes)]
            columns.append(jnp.concatenate([ref[start : start + 8] for start in starts], axis=0))
        return jnp.concatenate(columns, axis=1)

    img_re = of_part(straight_ref, 0) + of_part(turned_ref, 1)
    img_im = of_part(straight_ref, 1) - of_part(turned_ref, 0)
    sens_re, sens_im = sens_ref[:cells], sens_ref[cells:]
    out_ref[:cells] = sens_re * img_re + sens_im * img_im
    out_ref[cells:] = sens_re * img_im - sens_im * img_re


def add_kernel(own_ref, next_ref, across_ref, last_ref, out_ref):
    out_ref[...] = (own_ref[...] + across_ref[...]) + (next_ref[...] + last_ref[...])


def turn_kernel(
    lam_ref, one_ref, other_ref, vec_ref, sens_ref, table_ref, out_ref, image_ref, sums_ref, straight_ref, turned_ref
):
    cells2, width = vec_ref.shape
    cells = cells2 // 2
    vec = vec_ref[...]
    image = (one_ref[...] + other_ref[...]) + lam_ref[0] * vec
    image_ref[...] = image
    real, imag = coil_product(sens_ref, image[:cells], image[cells:])
    send_columns(real, imag, partial(pair_of, table_ref, 0), out_ref, straight_ref, turned_ref)
    norm = total(vec * vec)
    ratio = along(total(vec * image), norm)
    rest = image - ratio * vec
    row = lax.broadcasted_iota(jnp.int32, sums_ref.shape, 0)
    lanes = sums_ref.shape[1]
    sums_ref[...] = jnp.where(
        row == 0,
        row_of(norm, lanes),
        jnp.where(row == 1, row_of(ratio, lanes), row_of(total(rest * rest), lanes)),
    )


def last_kernel(in_ref, before_ref, energy_ref, sums_ref, by_depth_ref, rows_ref, out_ref):
    spec = spectrum(in_ref, rows_ref)
    cols = spec[0][0].shape[0]
    norm = energy_ref[0:1, 0:1]

    def before(at):
        return before_ref[2 * at * cols : (2 * at + 1) * cols], before_ref[(2 * at + 1) * cols : (2 * at + 2) * cols]

    def kernel(at):
        return by_depth_ref[at * cols : (at + 1) * cols]

    weight = 0.0
    for at, (real, imag) in enumerate(spec):
        real_0, imag_0 = before(at)
        weight = weight + kernel(at) * (real * real_0 + imag * imag_0)
    ratio = along(total(weight), norm)
    weight = 0.0
    for at, (real, imag) in enumerate(spec):
        real_0, imag_0 = before(at)
        real, imag = real - ratio * real_0, imag - ratio * imag_0
        weight = weight + kernel(at) * (real * real + imag * imag)
    lanes = out_ref.shape[1]
    values = [
        row_of(norm, lanes),
        row_of(ratio, lanes),
        row_of(total(weight), lanes),
        sums_ref[0:1],
        sums_ref[1:2],
        sums_ref[2:3],
    ]
    lane = lax.broadcasted_iota(jnp.int32, (1, lanes), 1)
    line = values[-1]
    for at, value in enumerate(values[:-1]):
        line = jnp.where(lane == at, value, line)
    out_ref[...] = jnp.broadcast_to(line, out_ref.shape)


def solution_kernel(lam_ref, all_ref, vec_ref, image_ref, out_ref):
    lam = lam_ref[0]
    every = all_ref[...]
    lane = lax.broadcasted_iota(jnp.int32, every.shape, 1)

    def column(at):
        return jnp.sum(jnp.where(lane == at, every, 0.0), axis=1, keepdims=True)

    def sum_of(values):
        return jnp.sum(values, axis=0, keepdims=True)

    deep_norm, deep_ratio, deep_rest, norms, ratios, rests = [column(at) for at in range(6)]
    norm = sum_of(norms) * 0.125
    curvature = sum_of(ratios * norms) * 0.125
    step = norm / curvature
    left, deep_left = 1.0 - step * ratios, 1.0 - step * deep_ratio
    fresh = sum_of(left * left * norms + step * step * rests) * 0.125
    cross = sum_of(ratios * norms * left - step * rests) * 0.125
    energy_now = sum_of(deep_left * deep_left * deep_norm + step * step * deep_rest)
    ratio = fresh / norm
    bent = energy_now + lam * fresh + ratio * (2.0 * cross + ratio * curvature)
    step_now = along(fresh, bent)
    vec = vec_ref[...]
    residual = vec - step * image_ref[...]
    out_ref[...] = step * vec + step_now * (residual + ratio * vec)


def call(kernel, shapes, places, scratch=(), limit=16):
    spaces = {"s": pltpu.SMEM, "v": pltpu.VMEM, "h": pltpu.HBM}
    outs = [jax.ShapeDtypeStruct(shape, F32) if isinstance(shape, tuple) else shape for shape in shapes]
    out_specs = [pl.BlockSpec(memory_space=pltpu.VMEM)] * len(shapes)
    return pl.pallas_call(
        kernel,
        out_shape=outs if len(outs) > 1 else outs[0],
        in_specs=[pl.BlockSpec(memory_space=spaces[place]) for place in places],
        out_specs=out_specs if len(outs) > 1 else out_specs[0],
        scratch_shapes=list(scratch),
        compiler_params=pltpu.CompilerParams(vmem_limit_bytes=limit * 2**20),
    )


def shards(cotangent, sensitivity, kernel, reg_weight):
    planes, rows, width = cotangent.shape[1:]
    slabs = lax.axis_size("slab")
    coils = lax.axis_size("coil")
    cols = kernel.shape[0]
    cells2 = 2 * planes * rows
    vec = cotangent.reshape(cells2, width)
    sens = sensitivity.reshape(cells2, width)
    filt = kernel.reshape(cols * kernel.shape[1], kernel.shape[2])
    table = halves(plane_table(width), 0)
    row_table = halves(rows_table(width, slabs, 1.0 / math.sqrt(2 * planes)), 0)
    lanes = planes * cols
    block = (slabs, 2 * rows, lanes)
    to_slabs = partial(lax.all_to_all, axis_name="slab", split_axis=0, concat_axis=0, tiled=True)
    dma = pltpu.SemaphoreType.DMA

    spaces = [pltpu.VMEM((cells2 * width // 128, 128), F32)] * 2
    sources = [pltpu.with_memory_space_constraint(array, pltpu.HBM) for array in (vec, sens, table, filt, row_table)]
    loaded = [pltpu.VMEM(array.shape, array.dtype) for array in sources]
    loaded[3] = pltpu.VMEM((filt.size // 128, 128), F32)
    sent, vec, sens, table, filt, row_table = call(
        start_kernel, [block, *loaded], "hhhhh", [dma((len(sources) + filt.shape[1] // 128 - 1,)), *spaces]
    )(*sources)
    got = to_slabs(sent)
    shapes = [block, (4 * lanes, 2 * width), (8, 128), (2 * lanes, 2 * width)]
    back, before, energy_now, filt = call(filter_kernel, shapes, "vvv", (), 32)(got, filt, row_table)
    home = to_slabs(back)
    term = call(image_kernel, [(cells2, width)], "vvv", spaces)(home, sens, table)

    chips = coils // 2

    def from_chip(shift):
        pairs = [
            (2 * chip + core, 2 * ((chip + shift) % chips) + core) for chip in range(chips) for core in range(2)
        ]
        return lax.ppermute(term, "coil", pairs)

    across = from_chip(2)
    pair = call(add_kernel, [term.shape], "vvvv")(term, from_chip(1), across, from_chip(3))
    other = lax.ppermute(pair, "coil", [(at, at ^ 1) for at in range(coils)])
    sent, image, sums = call(turn_kernel, [block, (cells2, width), (8, 128)], "svvvvv", spaces)(
        reg_weight, pair, other, vec, sens, table
    )
    got = to_slabs(sent)
    own = call(last_kernel, [(coils * slabs, 128)], "vvvvvv", (), 32)(
        got, before, energy_now, sums, filt, row_table
    )
    every = lax.all_to_all(own, ("coil", "slab"), 0, 0, tiled=True)
    result = call(solution_kernel, [(cells2, width)], "svvv")(reg_weight, every, vec, image)
    return result.reshape(cotangent.shape)


def solution(mesh):
    in_specs = (
        P(None, None, "slab", None),
        P("coil", None, None, "slab", None),
        P("slab", None, None),
        P(),
    )
    out_specs = P(None, None, "slab", None)
    return jax.shard_map(shards, mesh=mesh, in_specs=in_specs, out_specs=out_specs, check_vma=False)
```

```python
from functools import partial
import math

import jax
import jax.numpy as jnp
import numpy as np
from jax import lax
from jax.experimental import pallas as pl
from jax.experimental.pallas import tpu as pltpu
from jax.sharding import PartitionSpec as P

F32 = jnp.float32
BF16 = jnp.bfloat16
NN = ((1,), (0,))
NT = ((1,), (1,))


def dft(length):
    grid_size = 2 * length
    winding = np.outer(np.arange(length) + length // 2, np.arange(grid_size)) % grid_size
    return np.exp(-2j * np.pi * winding / grid_size) / math.sqrt(grid_size)


def halves(table, axis):
    high = table.astype(np.float32).astype(jnp.bfloat16)
    low = (table - high.astype(np.float64)).astype(np.float32).astype(jnp.bfloat16)
    return jnp.asarray(np.concatenate([high, low], axis=axis))


def pair_of(ref, axis):
    half = ref.shape[axis] // 2
    return (ref[:half], ref[half:]) if axis == 0 else (ref[:, :half], ref[:, half:])


def plane_table(length):
    table = dft(length)
    return np.concatenate([table.real, table.imag], axis=0)


def rows_table(length, slabs, scale):
    pairs = length // slabs // 2
    table = scale * dft(length)[:, :length].reshape(slabs, pairs, 2, length).transpose(2, 0, 1, 3)
    out = np.empty((2, slabs, 2, pairs, 2, length))
    out[:, :, 0, :, 0], out[:, :, 1, :, 0] = table.real, -table.imag
    out[:, :, 0, :, 1], out[:, :, 1, :, 1] = table.imag, table.real
    return out.reshape(2 * length, 2 * length)


def split(values):
    high = values.astype(BF16)
    low = (values - high.astype(F32)).astype(BF16)
    return high, low


def product(left, right, dims):
    dot = partial(lax.dot_general, dimension_numbers=(dims, ((), ())), preferred_element_type=F32)
    rows, cols = left[0].shape[0], right[0].shape[1 - dims[1][0]]
    if dims == NT and cols <= 128:
        both = dot(left[0], jnp.concatenate(right, axis=0))
        return (both[:, :cols] + both[:, cols:]) + dot(left[1], right[0])
    both = dot(jnp.concatenate(left, axis=0), right[0])
    return (both[:rows] + both[rows:]) + dot(left[0], right[1])


def exchange(tiles):
    count = len(tiles)
    width = tiles[0].shape[1]
    step = width // count
    group = lax.broadcasted_iota(jnp.int32, tiles[0].shape, 1) // step
    tiles = [pltpu.roll(tile, step * at, 1) if at else tile for at, tile in enumerate(tiles)]
    half = 1
    while half < count:
        later = (group // half) % 2 == 1
        tiles = [jnp.where(later, tiles[(at + half) % count], tiles[at]) for at in range(count)]
        half *= 2
    return [pltpu.roll(tiles[-at], width - step * at, 1) if at else tiles[0] for at in range(count)]


def coil_product(sens_ref, real, imag):
    rows = real.shape[0]
    sens_re, sens_im = sens_ref[:rows], sens_ref[rows:]
    return sens_re * real - sens_im * imag, sens_re * imag + sens_im * real


def send_columns(real, imag, table, out_ref, straight_ref, turned_ref):
    cells, width = real.shape
    rows, grid_size = 8, 2 * width
    planes, blocks = cells // rows, grid_size // 128
    for plane in range(planes):
        for lanes in range(0, width, 128):
            at = 2 * rows * plane + lanes // 128 * 2 * cells
            one = real[rows * plane : rows * (plane + 1), lanes : lanes + 128]
            other = imag[rows * plane : rows * (plane + 1), lanes : lanes + 128]
            straight_ref[at : at + rows], straight_ref[at + rows : at + 2 * rows] = one, other
            turned_ref[at : at + rows], turned_ref[at + rows : at + 2 * rows] = -other, one

    tiled = range(0, width // 128 * 2 * cells, 2 * cells)
    parts = [
        jnp.concatenate(
            [ref[pl.ds(at + parity, cells, stride=2), :] for ref in (straight_ref, turned_ref) for at in tiled], axis=1
        )
        for parity in range(2)
    ]
    dot = partial(jnp.dot, preferred_element_type=F32)
    pair = split(jnp.concatenate(parts, axis=0))
    spec = dot(jnp.concatenate(pair, axis=0), table(0))
    spec = (spec[: 2 * cells] + spec[2 * cells :]) + dot(pair[0], table(1))
    tiles = [
        jnp.concatenate(
            [
                spec[(parity * planes + plane) * rows :][:rows, block * 128 : (block + 1) * 128]
                for parity in range(2)
                for block in range(blocks)
            ],
            axis=0,
        )
        for plane in range(planes)
    ]
    tiles = exchange(tiles)
    for parity in range(2):
        for block in range(blocks):
            for at in range(planes):
                start = (parity * blocks + block) * rows
                out_ref[block * planes + at, parity * rows : (parity + 1) * rows, :] = tiles[at][
                    start : start + rows
                ]


def turn(value, power):
    real, imag = value
    power %= 16
    if power == 0:
        return real, imag
    if power == 4:
        return imag, -real
    if power == 8:
        return -real, -imag
    if power == 12:
        return -imag, real
    cos, sin = math.cos(math.pi * power / 8), -math.sin(math.pi * power / 8)
    return cos * real - sin * imag, cos * imag + sin * real


def plus(one, other):
    return one[0] + other[0], one[1] + other[1]


def minus(one, other):
    return one[0] - other[0], one[1] - other[1]


def four(values, power):
    even, even_off = plus(values[0], values[2]), minus(values[0], values[2])
    odd, odd_off = plus(values[1], values[3]), turn(minus(values[1], values[3]), power)
    return plus(even, odd), plus(even_off, odd_off), minus(even, odd), minus(even_off, odd_off)


def deepen(cells):
    out = [None] * 16
    for rest in range(4):
        folded = [plus(cells[at], turn(cells[at + 4], 4 * rest)) for at in range(4)]
        folded = [turn(value, (at + 4) * rest) for at, value in enumerate(folded)]
        for at, value in enumerate(four(folded, 4)):
            out[4 * at + rest] = value
    return out


def shallow(freqs):
    out = [None] * 8
    for rest in range(4):
        folded = four([freqs[4 * at + rest] for at in range(4)], -4)
        for at in range(4):
            value = turn(folded[at], -(at + 4) * rest)
            above = turn(value, -4 * rest)
            out[at] = value if rest == 0 else plus(out[at], value)
            out[at + 4] = above if rest == 0 else plus(out[at + 4], above)
    return out


def spectrum(in_ref, rows_ref):
    slabs, _, lanes = in_ref.shape
    high, low = pair_of(rows_ref, 0)
    length = high.shape[0] // 2
    parity = []
    for at in range(2):
        cells = in_ref[:, at * 8 : (at + 1) * 8, :].reshape(slabs * 8, lanes).T
        rows = slice(at * length, (at + 1) * length)
        parity.append(product(split(cells), (high[rows], low[rows]), NN))
    total_of, differ = parity[0] + parity[1], parity[0] - parity[1]
    real = jnp.concatenate([total_of[:, :length], differ[:, :length]], axis=1)
    imag = jnp.concatenate([total_of[:, length:], differ[:, length:]], axis=1)
    cols = lanes // 8
    return deepen([(real[at * cols : (at + 1) * cols], imag[at * cols : (at + 1) * cols]) for at in range(8)])


def at_depth(ref, at):
    cols = 16
    tiles = [
        ref[pl.ds(tile * 16 * cols + at, cols, stride=16), :] for tile in range(ref.shape[0] // (16 * cols))
    ]
    return jnp.concatenate(tiles, axis=1)


def total(values):
    return jnp.sum(jnp.sum(values, axis=0, keepdims=True), axis=1, keepdims=True)


def along(part, whole):
    return jnp.where(whole > 0.0, part / jnp.where(whole > 0.0, whole, 1.0), 0.0)


def row_of(value, lanes):
    return jnp.broadcast_to(value, (1, lanes))


def start_kernel(*refs):
    count = (len(refs) - 4) // 2
    sources, out_ref, loaded = refs[:count], refs[count], refs[count + 1 : 2 * count + 1]
    sems, *spaces = refs[2 * count + 1 :]
    vec_ref, sens_ref, table_ref = loaded[:3]
    half = table_ref.shape[0] // 2
    pairs = [(sources[at], loaded[at]) for at in range(2)]
    pairs += [(sources[2].at[pl.ds(at, half)], table_ref.at[pl.ds(at, half)]) for at in (0, half)]
    for source, target in zip(sources[3:], loaded[3:]):
        rows, lanes = source.shape[0], target.shape[1]
        for tile in range(source.shape[1] // lanes):
            pairs.append((source.at[:, pl.ds(tile * lanes, lanes)], target.at[pl.ds(tile * rows, rows)]))
    copies = [pltpu.make_async_copy(*pair, sems.at[at]) for at, pair in enumerate(pairs)]
    for copy in copies:
        copy.start()
    for copy in copies[:2]:
        copy.wait()
    cells = vec_ref.shape[0] // 2
    real, imag = coil_product(sens_ref, vec_ref[:cells], vec_ref[cells:])

    def table(part):
        copies[2 + part].wait()
        return table_ref[part * half : (part + 1) * half]

    send_columns(real, imag, table, out_ref, *spaces)
    for copy in copies[4:]:
        copy.wait()


def filter_kernel(in_ref, kernel_ref, rows_ref, out_ref, spec_ref, energy_ref, by_depth_ref):
    slabs, _, lanes = in_ref.shape
    spec = spectrum(in_ref, rows_ref)
    cols = lanes // 8
    weight = 0.0
    filtered = []
    for at, (real, imag) in enumerate(spec):
        spec_ref[2 * at * cols : (2 * at + 1) * cols] = real
        spec_ref[(2 * at + 1) * cols : (2 * at + 2) * cols] = imag
        kernel = at_depth(kernel_ref, at)
        by_depth_ref[at * cols : (at + 1) * cols] = kernel
        filtered.append((kernel * real, kernel * imag))
        weight = weight + (filtered[-1][0] * real + filtered[-1][1] * imag)
    energy_ref[...] = jnp.broadcast_to(total(weight), energy_ref.shape)
    planes = shallow(filtered)
    real, imag = [jnp.concatenate([plane[part] for plane in planes], axis=0) for part in range(2)]
    high, low = pair_of(rows_ref, 0)
    length = high.shape[0] // 2
    for at, join in enumerate((jnp.add, jnp.subtract)):
        folded = [join(part[:, :length], part[:, length:]) for part in (real, imag)]
        rows = slice(at * length, (at + 1) * length)
        back = product((high[rows], low[rows]), split(jnp.concatenate(folded, axis=1)), NT)
        out_ref[:, at * 8 : (at + 1) * 8, :] = back.reshape(slabs, 8, lanes)


def image_kernel(in_ref, sens_ref, table_ref, out_ref, straight_ref, turned_ref):
    slabs, _, lanes = in_ref.shape
    planes, blocks = 8, slabs // 8
    tiles = [
        jnp.concatenate(
            [
                in_ref[block * planes + at, part * 8 : (part + 1) * 8, :]
                for part in range(2)
                for block in range(blocks)
            ],
            axis=0,
        )
        for at in range(planes)
    ]
    tiles = exchange(tiles)
    spec = jnp.concatenate(
        [
            jnp.concatenate(
                [
                    tiles[plane][(part * blocks + block) * 8 : (part * blocks + block + 1) * 8]
                    for block in range(blocks)
                ],
                axis=1,
            )
            for part in range(2)
            for plane in range(planes)
        ],
        axis=0,
    )
    both = product(split(spec), pair_of(table_ref, 0), NT)
    by_real, by_imag = both[:, : both.shape[1] // 2], both[:, both.shape[1] // 2 :]
    cells = planes * 8
    tiled = range(by_real.shape[1] // 128)
    for parity in range(2):
        part = slice(parity * cells, (parity + 1) * cells)
        for tile in tiled:
            rows, tile_of = pl.ds(tile * 2 * cells + parity, cells, stride=2), slice(tile * 128, tile * 128 + 128)
            straight_ref[rows, :] = by_real[part, tile_of]
            turned_ref[rows, :] = by_imag[part, tile_of]

    def of_part(ref, part):
        columns = []
        for tile in tiled:
            starts = [tile * 2 * cells + 16 * plane + 8 * part for plane in range(planes)]
            columns.append(jnp.concatenate([ref[start : start + 8] for start in starts], axis=0))
        return jnp.concatenate(columns, axis=1)

    img_re = of_part(straight_ref, 0) + of_part(turned_ref, 1)
    img_im = of_part(straight_ref, 1) - of_part(turned_ref, 0)
    sens_re, sens_im = sens_ref[:cells], sens_ref[cells:]
    out_ref[:cells] = sens_re * img_re + sens_im * img_im
    out_ref[cells:] = sens_re * img_im - sens_im * img_re


def add_kernel(own_ref, next_ref, last_ref, across_ref, out_ref):
    out_ref[...] = (own_ref[...] + across_ref[...]) + (next_ref[...] + last_ref[...])


def turn_kernel(
    lam_ref, one_ref, other_ref, vec_ref, sens_ref, table_ref, out_ref, image_ref, sums_ref, straight_ref, turned_ref
):
    cells2, width = vec_ref.shape
    cells = cells2 // 2
    vec = vec_ref[...]
    image = (one_ref[...] + other_ref[...]) + lam_ref[0] * vec
    image_ref[...] = image
    real, imag = coil_product(sens_ref, image[:cells], image[cells:])
    send_columns(real, imag, pair_of(table_ref, 0).__getitem__, out_ref, straight_ref, turned_ref)
    norm = total(vec * vec)
    ratio = along(total(vec * image), norm)
    rest = image - ratio * vec
    row = lax.broadcasted_iota(jnp.int32, sums_ref.shape, 0)
    lanes = sums_ref.shape[1]
    sums_ref[...] = jnp.where(
        row == 0,
        row_of(norm, lanes),
        jnp.where(row == 1, row_of(ratio, lanes), row_of(total(rest * rest), lanes)),
    )


def last_kernel(in_ref, before_ref, energy_ref, sums_ref, by_depth_ref, rows_ref, out_ref):
    spec = spectrum(in_ref, rows_ref)
    cols = spec[0][0].shape[0]
    norm = energy_ref[0:1, 0:1]

    def before(at):
        return before_ref[2 * at * cols : (2 * at + 1) * cols], before_ref[(2 * at + 1) * cols : (2 * at + 2) * cols]

    def kernel(at):
        return by_depth_ref[at * cols : (at + 1) * cols]

    weight = 0.0
    for at, (real, imag) in enumerate(spec):
        real_0, imag_0 = before(at)
        weight = weight + kernel(at) * (real * real_0 + imag * imag_0)
    ratio = along(total(weight), norm)
    weight = 0.0
    for at, (real, imag) in enumerate(spec):
        real_0, imag_0 = before(at)
        real, imag = real - ratio * real_0, imag - ratio * imag_0
        weight = weight + kernel(at) * (real * real + imag * imag)
    lanes = out_ref.shape[1]
    values = [
        row_of(norm, lanes),
        row_of(ratio, lanes),
        row_of(total(weight), lanes),
        sums_ref[0:1],
        sums_ref[1:2],
        sums_ref[2:3],
    ]
    lane = lax.broadcasted_iota(jnp.int32, (1, lanes), 1)
    line = values[-1]
    for at, value in enumerate(values[:-1]):
        line = jnp.where(lane == at, value, line)
    out_ref[...] = jnp.broadcast_to(line, out_ref.shape)


def solution_kernel(lam_ref, all_ref, vec_ref, image_ref, out_ref):
    lam = lam_ref[0]
    every = all_ref[...]
    lane = lax.broadcasted_iota(jnp.int32, every.shape, 1)

    def column(at):
        return jnp.sum(jnp.where(lane == at, every, 0.0), axis=1, keepdims=True)

    def sum_of(values):
        return jnp.sum(values, axis=0, keepdims=True)

    deep_norm, deep_ratio, deep_rest, norms, ratios, rests = [column(at) for at in range(6)]
    norm = sum_of(norms) * 0.125
    curvature = sum_of(ratios * norms) * 0.125
    step = norm / curvature
    left, deep_left = 1.0 - step * ratios, 1.0 - step * deep_ratio
    fresh = sum_of(left * left * norms + step * step * rests) * 0.125
    cross = sum_of(ratios * norms * left - step * rests) * 0.125
    energy_now = sum_of(deep_left * deep_left * deep_norm + step * step * deep_rest)
    ratio = fresh / norm
    bent = energy_now + lam * fresh + ratio * (2.0 * cross + ratio * curvature)
    step_now = along(fresh, bent)
    vec = vec_ref[...]
    residual = vec - step * image_ref[...]
    out_ref[...] = step * vec + step_now * (residual + ratio * vec)


def call(kernel, shapes, places, scratch=(), limit=16):
    spaces = {"s": pltpu.SMEM, "v": pltpu.VMEM, "h": pltpu.HBM}
    outs = [jax.ShapeDtypeStruct(shape, F32) if isinstance(shape, tuple) else shape for shape in shapes]
    out_specs = [pl.BlockSpec(memory_space=pltpu.VMEM)] * len(shapes)
    return pl.pallas_call(
        kernel,
        out_shape=outs if len(outs) > 1 else outs[0],
        in_specs=[pl.BlockSpec(memory_space=spaces[place]) for place in places],
        out_specs=out_specs if len(outs) > 1 else out_specs[0],
        scratch_shapes=list(scratch),
        compiler_params=pltpu.CompilerParams(vmem_limit_bytes=limit * 2**20),
    )


def shards(cotangent, sensitivity, kernel, reg_weight):
    planes, rows, width = cotangent.shape[1:]
    slabs = lax.axis_size("slab")
    coils = lax.axis_size("coil")
    cols = kernel.shape[0]
    cells2 = 2 * planes * rows
    vec = cotangent.reshape(cells2, width)
    sens = sensitivity.reshape(cells2, width)
    filt = kernel.reshape(cols * kernel.shape[1], kernel.shape[2])
    table = halves(plane_table(width), 0)
    row_table = halves(rows_table(width, slabs, 1.0 / math.sqrt(2 * planes)), 0)
    lanes = planes * cols
    block = (slabs, 2 * rows, lanes)
    to_slabs = partial(lax.all_to_all, axis_name="slab", split_axis=0, concat_axis=0, tiled=True)
    dma = pltpu.SemaphoreType.DMA

    spaces = [pltpu.VMEM((cells2 * width // 128, 128), F32)] * 2
    sources = [pltpu.with_memory_space_constraint(array, pltpu.HBM) for array in (vec, sens, table, filt, row_table)]
    loaded = [pltpu.VMEM(array.shape, array.dtype) for array in sources]
    loaded[3] = pltpu.VMEM((filt.size // 128, 128), F32)
    sent, vec, sens, table, filt, row_table = call(
        start_kernel, [block, *loaded], "hhhhh", [dma((len(sources) + filt.shape[1] // 128,)), *spaces]
    )(*sources)
    got = to_slabs(sent)
    shapes = [block, (4 * lanes, 2 * width), (8, 128), (2 * lanes, 2 * width)]
    back, before, energy_now, filt = call(filter_kernel, shapes, "vvv", (), 32)(got, filt, row_table)
    home = to_slabs(back)
    term = call(image_kernel, [(cells2, width)], "vvv", spaces)(home, sens, table)

    chips = coils // 2

    def from_chip(shift):
        pairs = [
            (2 * chip + core, 2 * ((chip + shift) % chips) + core) for chip in range(chips) for core in range(2)
        ]
        return lax.ppermute(term, "coil", pairs)

    pair = call(add_kernel, [term.shape], "vvvv")(term, *[from_chip(shift) for shift in (1, 3, 2)])
    other = lax.ppermute(pair, "coil", [(at, at ^ 1) for at in range(coils)])
    sent, image, sums = call(turn_kernel, [block, (cells2, width), (8, 128)], "svvvvv", spaces)(
        reg_weight, pair, other, vec, sens, table
    )
    got = to_slabs(sent)
    own = call(last_kernel, [(coils * slabs, 128)], "vvvvvv", (), 32)(
        got, before, energy_now, sums, filt, row_table
    )
    every = lax.all_to_all(own, ("coil", "slab"), 0, 0, tiled=True)
    result = call(solution_kernel, [(cells2, width)], "svvv")(reg_weight, every, vec, image)
    return result.reshape(cotangent.shape)


def solution(mesh):
    in_specs = (
        P(None, None, "slab", None),
        P("coil", None, None, "slab", None),
        P("slab", None, None),
        P(),
    )
    out_specs = P(None, None, "slab", None)
    return jax.shard_map(shards, mesh=mesh, in_specs=in_specs, out_specs=out_specs, check_vma=False)
```

```python
from functools import partial
import math

import jax
import jax.numpy as jnp
import numpy as np
from jax import lax
from jax.experimental import pallas as pl
from jax.experimental.pallas import tpu as pltpu
from jax.sharding import PartitionSpec as P

F32 = jnp.float32
BF16 = jnp.bfloat16
NN = ((1,), (0,))
NT = ((1,), (1,))


def dft(length):
    grid_size = 2 * length
    winding = np.outer(np.arange(length) + length // 2, np.arange(grid_size)) % grid_size
    return np.exp(-2j * np.pi * winding / grid_size) / math.sqrt(grid_size)


def halves(table, axis):
    high = table.astype(np.float32).astype(jnp.bfloat16)
    low = (table - high.astype(np.float64)).astype(np.float32).astype(jnp.bfloat16)
    return jnp.asarray(np.concatenate([high, low], axis=axis))


def pair_of(ref, axis):
    half = ref.shape[axis] // 2
    return (ref[:half], ref[half:]) if axis == 0 else (ref[:, :half], ref[:, half:])


def plane_table(length):
    table = dft(length)
    return np.concatenate([table.real, table.imag], axis=0)


def rows_table(length, slabs, scale):
    pairs = length // slabs // 2
    table = scale * dft(length)[:, :length].reshape(slabs, pairs, 2, length).transpose(2, 0, 1, 3)
    out = np.empty((2, slabs, 2, pairs, 2, length))
    out[:, :, 0, :, 0], out[:, :, 1, :, 0] = table.real, -table.imag
    out[:, :, 0, :, 1], out[:, :, 1, :, 1] = table.imag, table.real
    return out.reshape(2 * length, 2 * length)


def split(values):
    high = values.astype(BF16)
    low = (values - high.astype(F32)).astype(BF16)
    return high, low


def product(left, right, dims):
    dot = partial(lax.dot_general, dimension_numbers=(dims, ((), ())), preferred_element_type=F32)
    rows, cols = left[0].shape[0], right[0].shape[1 - dims[1][0]]
    if dims == NT and cols <= 128:
        both = dot(left[0], jnp.concatenate(right, axis=0))
        return (both[:, :cols] + both[:, cols:]) + dot(left[1], right[0])
    both = dot(jnp.concatenate(left, axis=0), right[0])
    return (both[:rows] + both[rows:]) + dot(left[0], right[1])


def exchange(tiles):
    count = len(tiles)
    width = tiles[0].shape[1]
    step = width // count
    group = lax.broadcasted_iota(jnp.int32, tiles[0].shape, 1) // step
    tiles = [pltpu.roll(tile, step * at, 1) if at else tile for at, tile in enumerate(tiles)]
    half = 1
    while half < count:
        later = (group // half) % 2 == 1
        tiles = [jnp.where(later, tiles[(at + half) % count], tiles[at]) for at in range(count)]
        half *= 2
    return [pltpu.roll(tiles[-at], width - step * at, 1) if at else tiles[0] for at in range(count)]


def coil_product(sens_ref, real, imag):
    rows = real.shape[0]
    sens_re, sens_im = sens_ref[:rows], sens_ref[rows:]
    return sens_re * real - sens_im * imag, sens_re * imag + sens_im * real


def send_columns(real, imag, table, out_ref, straight_ref, turned_ref):
    cells, width = real.shape
    rows, grid_size = 8, 2 * width
    planes, blocks = cells // rows, grid_size // 128
    for plane in range(planes):
        for lanes in range(0, width, 128):
            at = 2 * rows * plane + lanes // 128 * 2 * cells
            one = real[rows * plane : rows * (plane + 1), lanes : lanes + 128]
            other = imag[rows * plane : rows * (plane + 1), lanes : lanes + 128]
            straight_ref[at : at + rows], straight_ref[at + rows : at + 2 * rows] = one, other
            turned_ref[at : at + rows], turned_ref[at + rows : at + 2 * rows] = -other, one

    tiled = range(0, width // 128 * 2 * cells, 2 * cells)
    parts = [
        jnp.concatenate(
            [ref[pl.ds(at + parity, cells, stride=2), :] for ref in (straight_ref, turned_ref) for at in tiled], axis=1
        )
        for parity in range(2)
    ]
    dot = partial(jnp.dot, preferred_element_type=F32)
    pair = split(jnp.concatenate(parts, axis=0))
    spec = dot(jnp.concatenate(pair, axis=0), table(0))
    spec = (spec[: 2 * cells] + spec[2 * cells :]) + dot(pair[0], table(1))
    tiles = [
        jnp.concatenate(
            [
                spec[(parity * planes + plane) * rows :][:rows, block * 128 : (block + 1) * 128]
                for parity in range(2)
                for block in range(blocks)
            ],
            axis=0,
        )
        for plane in range(planes)
    ]
    tiles = exchange(tiles)
    for parity in range(2):
        for block in range(blocks):
            for at in range(planes):
                start = (parity * blocks + block) * rows
                out_ref[block * planes + at, parity * rows : (parity + 1) * rows, :] = tiles[at][
                    start : start + rows
                ]


def turn(value, power):
    real, imag = value
    power %= 16
    if power == 0:
        return real, imag
    if power == 4:
        return imag, -real
    if power == 8:
        return -real, -imag
    if power == 12:
        return -imag, real
    cos, sin = math.cos(math.pi * power / 8), -math.sin(math.pi * power / 8)
    return cos * real - sin * imag, cos * imag + sin * real


def plus(one, other):
    return one[0] + other[0], one[1] + other[1]


def minus(one, other):
    return one[0] - other[0], one[1] - other[1]


def four(values, power):
    even, even_off = plus(values[0], values[2]), minus(values[0], values[2])
    odd, odd_off = plus(values[1], values[3]), turn(minus(values[1], values[3]), power)
    return plus(even, odd), plus(even_off, odd_off), minus(even, odd), minus(even_off, odd_off)


def deepen(cells):
    out = [None] * 16
    for rest in range(4):
        folded = [plus(cells[at], turn(cells[at + 4], 4 * rest)) for at in range(4)]
        folded = [turn(value, (at + 4) * rest) for at, value in enumerate(folded)]
        for at, value in enumerate(four(folded, 4)):
            out[4 * at + rest] = value
    return out


def shallow(freqs):
    out = [None] * 8
    for rest in range(4):
        folded = four([freqs[4 * at + rest] for at in range(4)], -4)
        for at in range(4):
            value = turn(folded[at], -(at + 4) * rest)
            above = turn(value, -4 * rest)
            out[at] = value if rest == 0 else plus(out[at], value)
            out[at + 4] = above if rest == 0 else plus(out[at + 4], above)
    return out


def spectrum(in_ref, rows_ref):
    slabs, _, lanes = in_ref.shape
    high, low = pair_of(rows_ref, 0)
    length = high.shape[0] // 2
    parity = []
    for at in range(2):
        cells = in_ref[:, at * 8 : (at + 1) * 8, :].reshape(slabs * 8, lanes).T
        rows = slice(at * length, (at + 1) * length)
        parity.append(product(split(cells), (high[rows], low[rows]), NN))
    total_of, differ = parity[0] + parity[1], parity[0] - parity[1]
    real = jnp.concatenate([total_of[:, :length], differ[:, :length]], axis=1)
    imag = jnp.concatenate([total_of[:, length:], differ[:, length:]], axis=1)
    cols = lanes // 8
    return deepen([(real[at * cols : (at + 1) * cols], imag[at * cols : (at + 1) * cols]) for at in range(8)])


def at_depth(ref, at):
    cols = 16
    tiles = [
        ref[pl.ds(tile * 16 * cols + at, cols, stride=16), :] for tile in range(ref.shape[0] // (16 * cols))
    ]
    return jnp.concatenate(tiles, axis=1)


def total(values):
    return jnp.sum(jnp.sum(values, axis=0, keepdims=True), axis=1, keepdims=True)


def along(part, whole):
    return jnp.where(whole > 0.0, part / jnp.where(whole > 0.0, whole, 1.0), 0.0)


def row_of(value, lanes):
    return jnp.broadcast_to(value, (1, lanes))


def start_kernel(*refs):
    count = (len(refs) - 7) // 2
    sources, core_hbm, out_ref, loaded = refs[:count], refs[count], refs[count + 1], refs[count + 2 : 2 * count + 2]
    core_ref, sems, core_smem, *spaces = refs[2 * count + 2 :]
    vec_ref, sens_ref, table_ref = loaded[:3]
    half = table_ref.shape[0] // 2
    pairs = [(sources[at], loaded[at]) for at in range(2)]
    pairs += [(sources[2].at[pl.ds(at, half)], table_ref.at[pl.ds(at, half)]) for at in (0, half)]
    for source, target in zip(sources[3:], loaded[3:]):
        rows, lanes = source.shape[0], target.shape[1]
        for tile in range(source.shape[1] // lanes):
            pairs.append((source.at[:, pl.ds(tile * lanes, lanes)], target.at[pl.ds(tile * rows, rows)]))
    pairs.append((core_hbm, core_smem))
    copies = [pltpu.make_async_copy(*pair, sems.at[at]) for at, pair in enumerate(pairs)]
    for copy in copies:
        copy.start()
    for copy in copies[:2]:
        copy.wait()
    cells = vec_ref.shape[0] // 2
    real, imag = coil_product(sens_ref, vec_ref[:cells], vec_ref[cells:])

    def table(part):
        copies[2 + part].wait()
        return table_ref[part * half : (part + 1) * half]

    send_columns(real, imag, table, out_ref, *spaces)
    for copy in copies[4:]:
        copy.wait()
    core_ref[...] = jnp.full(core_ref.shape, core_smem[0], F32)


def filter_kernel(in_ref, kernel_ref, rows_ref, out_ref, spec_ref, energy_ref, by_depth_ref):
    slabs, _, lanes = in_ref.shape
    spec = spectrum(in_ref, rows_ref)
    cols = lanes // 8
    weight = 0.0
    filtered = []
    for at, (real, imag) in enumerate(spec):
        spec_ref[2 * at * cols : (2 * at + 1) * cols] = real
        spec_ref[(2 * at + 1) * cols : (2 * at + 2) * cols] = imag
        kernel = at_depth(kernel_ref, at)
        by_depth_ref[at * cols : (at + 1) * cols] = kernel
        filtered.append((kernel * real, kernel * imag))
        weight = weight + (filtered[-1][0] * real + filtered[-1][1] * imag)
    energy_ref[...] = jnp.broadcast_to(total(weight), energy_ref.shape)
    planes = shallow(filtered)
    real, imag = [jnp.concatenate([plane[part] for plane in planes], axis=0) for part in range(2)]
    high, low = pair_of(rows_ref, 0)
    length = high.shape[0] // 2
    for at, join in enumerate((jnp.add, jnp.subtract)):
        folded = [join(part[:, :length], part[:, length:]) for part in (real, imag)]
        rows = slice(at * length, (at + 1) * length)
        back = product((high[rows], low[rows]), split(jnp.concatenate(folded, axis=1)), NT)
        out_ref[:, at * 8 : (at + 1) * 8, :] = back.reshape(slabs, 8, lanes)


def image_kernel(in_ref, sens_ref, table_ref, out_ref, straight_ref, turned_ref):
    slabs, _, lanes = in_ref.shape
    planes, blocks = 8, slabs // 8
    tiles = [
        jnp.concatenate(
            [
                in_ref[block * planes + at, part * 8 : (part + 1) * 8, :]
                for part in range(2)
                for block in range(blocks)
            ],
            axis=0,
        )
        for at in range(planes)
    ]
    tiles = exchange(tiles)
    spec = jnp.concatenate(
        [
            jnp.concatenate(
                [
                    tiles[plane][(part * blocks + block) * 8 : (part * blocks + block + 1) * 8]
                    for block in range(blocks)
                ],
                axis=1,
            )
            for part in range(2)
            for plane in range(planes)
        ],
        axis=0,
    )
    both = product(split(spec), pair_of(table_ref, 0), NT)
    by_real, by_imag = both[:, : both.shape[1] // 2], both[:, both.shape[1] // 2 :]
    cells = planes * 8
    tiled = range(by_real.shape[1] // 128)
    for parity in range(2):
        part = slice(parity * cells, (parity + 1) * cells)
        for tile in tiled:
            rows, tile_of = pl.ds(tile * 2 * cells + parity, cells, stride=2), slice(tile * 128, tile * 128 + 128)
            straight_ref[rows, :] = by_real[part, tile_of]
            turned_ref[rows, :] = by_imag[part, tile_of]

    def of_part(ref, part):
        columns = []
        for tile in tiled:
            starts = [tile * 2 * cells + 16 * plane + 8 * part for plane in range(planes)]
            columns.append(jnp.concatenate([ref[start : start + 8] for start in starts], axis=0))
        return jnp.concatenate(columns, axis=1)

    img_re = of_part(straight_ref, 0) + of_part(turned_ref, 1)
    img_im = of_part(straight_ref, 1) - of_part(turned_ref, 0)
    sens_re, sens_im = sens_ref[:cells], sens_ref[cells:]
    out_ref[:cells] = sens_re * img_re + sens_im * img_im
    out_ref[cells:] = sens_re * img_im - sens_im * img_re


def is_first(core_ref, shape):
    return jnp.broadcast_to(core_ref[0:1, 0:1], shape) == 0.0


def pair_kernel(core_ref, own_ref, other_ref, out_ref, half_ref):
    rows = half_ref.shape[0]
    both = own_ref[...] + other_ref[...]
    out_ref[...] = both
    half_ref[...] = jnp.where(is_first(core_ref, half_ref.shape), both[:rows], both[rows:])


def turn_kernel(
    core_ref,
    lam_ref,
    pair_ref,
    near_ref,
    other_near_ref,
    far_ref,
    other_far_ref,
    vec_ref,
    sens_ref,
    table_ref,
    out_ref,
    image_ref,
    sums_ref,
    straight_ref,
    turned_ref,
):
    cells2, width = vec_ref.shape
    cells = cells2 // 2
    vec = vec_ref[...]
    first = is_first(core_ref, far_ref.shape)
    far, other_far = far_ref[...], other_far_ref[...]
    across = jnp.concatenate([jnp.where(first, far, other_far), jnp.where(first, other_far, far)], axis=0)
    image = ((pair_ref[...] + across) + (near_ref[...] + other_near_ref[...])) + lam_ref[0] * vec
    image_ref[...] = image
    real, imag = coil_product(sens_ref, image[:cells], image[cells:])
    send_columns(real, imag, pair_of(table_ref, 0).__getitem__, out_ref, straight_ref, turned_ref)
    norm = total(vec * vec)
    ratio = along(total(vec * image), norm)
    rest = image - ratio * vec
    row = lax.broadcasted_iota(jnp.int32, sums_ref.shape, 0)
    lanes = sums_ref.shape[1]
    sums_ref[...] = jnp.where(
        row == 0,
        row_of(norm, lanes),
        jnp.where(row == 1, row_of(ratio, lanes), row_of(total(rest * rest), lanes)),
    )


def last_kernel(in_ref, before_ref, energy_ref, sums_ref, by_depth_ref, rows_ref, out_ref):
    spec = spectrum(in_ref, rows_ref)
    cols = spec[0][0].shape[0]
    norm = energy_ref[0:1, 0:1]

    def before(at):
        return before_ref[2 * at * cols : (2 * at + 1) * cols], before_ref[(2 * at + 1) * cols : (2 * at + 2) * cols]

    def kernel(at):
        return by_depth_ref[at * cols : (at + 1) * cols]

    weight = 0.0
    for at, (real, imag) in enumerate(spec):
        real_0, imag_0 = before(at)
        weight = weight + kernel(at) * (real * real_0 + imag * imag_0)
    ratio = along(total(weight), norm)
    weight = 0.0
    for at, (real, imag) in enumerate(spec):
        real_0, imag_0 = before(at)
        real, imag = real - ratio * real_0, imag - ratio * imag_0
        weight = weight + kernel(at) * (real * real + imag * imag)
    lanes = out_ref.shape[1]
    values = [
        row_of(norm, lanes),
        row_of(ratio, lanes),
        row_of(total(weight), lanes),
        sums_ref[0:1],
        sums_ref[1:2],
        sums_ref[2:3],
    ]
    lane = lax.broadcasted_iota(jnp.int32, (1, lanes), 1)
    line = values[-1]
    for at, value in enumerate(values[:-1]):
        line = jnp.where(lane == at, value, line)
    out_ref[...] = jnp.broadcast_to(line, out_ref.shape)


def solution_kernel(lam_ref, all_ref, vec_ref, image_ref, out_ref):
    lam = lam_ref[0]
    every = all_ref[...]
    lane = lax.broadcasted_iota(jnp.int32, every.shape, 1)

    def column(at):
        return jnp.sum(jnp.where(lane == at, every, 0.0), axis=1, keepdims=True)

    def sum_of(values):
        return jnp.sum(values, axis=0, keepdims=True)

    deep_norm, deep_ratio, deep_rest, norms, ratios, rests = [column(at) for at in range(6)]
    norm = sum_of(norms) * 0.125
    curvature = sum_of(ratios * norms) * 0.125
    step = norm / curvature
    left, deep_left = 1.0 - step * ratios, 1.0 - step * deep_ratio
    fresh = sum_of(left * left * norms + step * step * rests) * 0.125
    cross = sum_of(ratios * norms * left - step * rests) * 0.125
    energy_now = sum_of(deep_left * deep_left * deep_norm + step * step * deep_rest)
    ratio = fresh / norm
    bent = energy_now + lam * fresh + ratio * (2.0 * cross + ratio * curvature)
    step_now = along(fresh, bent)
    vec = vec_ref[...]
    residual = vec - step * image_ref[...]
    out_ref[...] = step * vec + step_now * (residual + ratio * vec)


def call(kernel, shapes, places, scratch=(), limit=16):
    spaces = {"s": pltpu.SMEM, "v": pltpu.VMEM, "h": pltpu.HBM}
    outs = [jax.ShapeDtypeStruct(shape, F32) if isinstance(shape, tuple) else shape for shape in shapes]
    out_specs = [pl.BlockSpec(memory_space=pltpu.VMEM)] * len(shapes)
    return pl.pallas_call(
        kernel,
        out_shape=outs if len(outs) > 1 else outs[0],
        in_specs=[pl.BlockSpec(memory_space=spaces[place]) for place in places],
        out_specs=out_specs if len(outs) > 1 else out_specs[0],
        scratch_shapes=list(scratch),
        compiler_params=pltpu.CompilerParams(vmem_limit_bytes=limit * 2**20),
    )


def shards(cotangent, sensitivity, kernel, reg_weight):
    planes, rows, width = cotangent.shape[1:]
    slabs = lax.axis_size("slab")
    coils = lax.axis_size("coil")
    cols = kernel.shape[0]
    cells2 = 2 * planes * rows
    vec = cotangent.reshape(cells2, width)
    sens = sensitivity.reshape(cells2, width)
    filt = kernel.reshape(cols * kernel.shape[1], kernel.shape[2])
    table = halves(plane_table(width), 0)
    row_table = halves(rows_table(width, slabs, 1.0 / math.sqrt(2 * planes)), 0)
    lanes = planes * cols
    core = (lax.axis_index("coil") % 2).astype(F32).reshape(1)
    block = (slabs, 2 * rows, lanes)
    to_slabs = partial(lax.all_to_all, axis_name="slab", split_axis=0, concat_axis=0, tiled=True)
    dma = pltpu.SemaphoreType.DMA

    spaces = [pltpu.VMEM((cells2 * width // 128, 128), F32)] * 2
    sources = [pltpu.with_memory_space_constraint(array, pltpu.HBM) for array in (vec, sens, table, filt, row_table)]
    loaded = [pltpu.VMEM(array.shape, array.dtype) for array in sources]
    loaded[3] = pltpu.VMEM((filt.size // 128, 128), F32)
    core = pltpu.with_memory_space_constraint(core, pltpu.HBM)
    sems = dma((len(sources) + filt.shape[1] // 128 + 1,))
    sent, vec, sens, table, filt, row_table, core = call(
        start_kernel,
        [block, *loaded, pltpu.VMEM((8, 128), F32)],
        "hhhhhh",
        [sems, pltpu.SMEM((1,), F32), *spaces],
    )(*sources, core)
    got = to_slabs(sent)
    shapes = [block, (4 * lanes, 2 * width), (8, 128), (2 * lanes, 2 * width)]
    back, before, energy_now, filt = call(filter_kernel, shapes, "vvv", (), 32)(got, filt, row_table)
    home = to_slabs(back)
    term = call(image_kernel, [(cells2, width)], "vvv", spaces)(home, sens, table)

    chips = coils // 2

    def moved(values, core_flip, *shifts):
        pairs = [
            (2 * chip + at, 2 * ((chip + shifts[at]) % chips) + (at ^ core_flip)) for chip in range(chips) for at in (0, 1)
        ]
        return lax.ppermute(values, "coil", pairs)

    halves_of = [pltpu.VMEM((cells2, width), F32), pltpu.VMEM((cells2 // 2, width), F32)]
    pair, half = call(pair_kernel, halves_of, "vvv")(core, term, moved(term, 1, 0, 0))
    near, far = moved(pair, 0, 1, chips - 1), moved(half, 0, 2, 2)
    sent, image, sums = call(turn_kernel, [block, (cells2, width), (8, 128)], "vsvvvvvvvv", spaces)(
        core, reg_weight, pair, near, moved(near, 1, 0, 0), far, moved(far, 1, 0, 0), vec, sens, table
    )
    got = to_slabs(sent)
    own = call(last_kernel, [(coils * slabs, 128)], "vvvvvv", (), 32)(
        got, before, energy_now, sums, filt, row_table
    )
    every = lax.all_to_all(own, ("coil", "slab"), 0, 0, tiled=True)
    result = call(solution_kernel, [(cells2, width)], "svvv")(reg_weight, every, vec, image)
    return result.reshape(cotangent.shape)


def solution(mesh):
    in_specs = (
        P(None, None, "slab", None),
        P("coil", None, None, "slab", None),
        P("slab", None, None),
        P(),
    )
    out_specs = P(None, None, "slab", None)
    return jax.shard_map(shards, mesh=mesh, in_specs=in_specs, out_specs=out_specs, check_vma=False)
```

```python
from functools import partial
import math

import jax
import jax.numpy as jnp
import numpy as np
from jax import lax
from jax.experimental import pallas as pl
from jax.experimental.pallas import tpu as pltpu
from jax.sharding import PartitionSpec as P

F32 = jnp.float32
BF16 = jnp.bfloat16
NN = ((1,), (0,))
NT = ((1,), (1,))


def dft(length):
    grid_size = 2 * length
    winding = np.outer(np.arange(length) + length // 2, np.arange(grid_size)) % grid_size
    return np.exp(-2j * np.pi * winding / grid_size) / math.sqrt(grid_size)


def halves(table, axis):
    high = table.astype(np.float32).astype(jnp.bfloat16)
    low = (table - high.astype(np.float64)).astype(np.float32).astype(jnp.bfloat16)
    return jnp.asarray(np.concatenate([high, low], axis=axis))


def pair_of(ref, axis):
    half = ref.shape[axis] // 2
    return (ref[:half], ref[half:]) if axis == 0 else (ref[:, :half], ref[:, half:])


def plane_table(length):
    table = dft(length)
    return np.concatenate([table.real, table.imag], axis=0)


def rows_table(length, slabs, scale):
    pairs = length // slabs // 2
    table = scale * dft(length)[:, :length].reshape(slabs, pairs, 2, length).transpose(2, 0, 1, 3)
    out = np.empty((2, slabs, 2, pairs, 2, length))
    out[:, :, 0, :, 0], out[:, :, 1, :, 0] = table.real, -table.imag
    out[:, :, 0, :, 1], out[:, :, 1, :, 1] = table.imag, table.real
    return out.reshape(2 * length, 2 * length)


def split(values):
    high = values.astype(BF16)
    low = (values - high.astype(F32)).astype(BF16)
    return high, low


def product(left, right, dims):
    dot = partial(lax.dot_general, dimension_numbers=(dims, ((), ())), preferred_element_type=F32)
    rows, cols = left[0].shape[0], right[0].shape[1 - dims[1][0]]
    if dims == NT and cols <= 128:
        both = dot(left[0], jnp.concatenate(right, axis=0))
        return (both[:, :cols] + both[:, cols:]) + dot(left[1], right[0])
    both = dot(jnp.concatenate(left, axis=0), right[0])
    return (both[:rows] + both[rows:]) + dot(left[0], right[1])


def exchange(tiles):
    count = len(tiles)
    width = tiles[0].shape[1]
    step = width // count
    group = lax.broadcasted_iota(jnp.int32, tiles[0].shape, 1) // step
    tiles = [pltpu.roll(tile, step * at, 1) if at else tile for at, tile in enumerate(tiles)]
    half = 1
    while half < count:
        later = (group // half) % 2 == 1
        tiles = [jnp.where(later, tiles[(at + half) % count], tiles[at]) for at in range(count)]
        half *= 2
    return [pltpu.roll(tiles[-at], width - step * at, 1) if at else tiles[0] for at in range(count)]


def coil_product(sens_ref, real, imag):
    rows = real.shape[0]
    sens_re, sens_im = sens_ref[:rows], sens_ref[rows:]
    return sens_re * real - sens_im * imag, sens_re * imag + sens_im * real


def send_columns(real, imag, table, out_ref, straight_ref, turned_ref):
    cells, width = real.shape
    rows, grid_size = 8, 2 * width
    planes, blocks = cells // rows, grid_size // 128
    for plane in range(planes):
        for lanes in range(0, width, 128):
            at = 2 * rows * plane + lanes // 128 * 2 * cells
            one = real[rows * plane : rows * (plane + 1), lanes : lanes + 128]
            other = imag[rows * plane : rows * (plane + 1), lanes : lanes + 128]
            straight_ref[at : at + rows], straight_ref[at + rows : at + 2 * rows] = one, other
            turned_ref[at : at + rows], turned_ref[at + rows : at + 2 * rows] = -other, one

    tiled = range(0, width // 128 * 2 * cells, 2 * cells)
    parts = [
        jnp.concatenate(
            [ref[pl.ds(at + parity, cells, stride=2), :] for ref in (straight_ref, turned_ref) for at in tiled], axis=1
        )
        for parity in range(2)
    ]
    dot = partial(jnp.dot, preferred_element_type=F32)
    pair = split(jnp.concatenate(parts, axis=0))
    spec = dot(jnp.concatenate(pair, axis=0), table(0))
    spec = (spec[: 2 * cells] + spec[2 * cells :]) + dot(pair[0], table(1))
    tiles = [
        jnp.concatenate(
            [
                spec[(parity * planes + plane) * rows :][:rows, block * 128 : (block + 1) * 128]
                for parity in range(2)
                for block in range(blocks)
            ],
            axis=0,
        )
        for plane in range(planes)
    ]
    tiles = exchange(tiles)
    for parity in range(2):
        for block in range(blocks):
            for at in range(planes):
                start = (parity * blocks + block) * rows
                out_ref[block * planes + at, parity * rows : (parity + 1) * rows, :] = tiles[at][
                    start : start + rows
                ]


def turn(value, power):
    real, imag = value
    power %= 16
    if power == 0:
        return real, imag
    if power == 4:
        return imag, -real
    if power == 8:
        return -real, -imag
    if power == 12:
        return -imag, real
    cos, sin = math.cos(math.pi * power / 8), -math.sin(math.pi * power / 8)
    return cos * real - sin * imag, cos * imag + sin * real


def plus(one, other):
    return one[0] + other[0], one[1] + other[1]


def minus(one, other):
    return one[0] - other[0], one[1] - other[1]


def four(values, power):
    even, even_off = plus(values[0], values[2]), minus(values[0], values[2])
    odd, odd_off = plus(values[1], values[3]), turn(minus(values[1], values[3]), power)
    return plus(even, odd), plus(even_off, odd_off), minus(even, odd), minus(even_off, odd_off)


def deepen(cells):
    out = [None] * 16
    for rest in range(4):
        folded = [plus(cells[at], turn(cells[at + 4], 4 * rest)) for at in range(4)]
        folded = [turn(value, (at + 4) * rest) for at, value in enumerate(folded)]
        for at, value in enumerate(four(folded, 4)):
            out[4 * at + rest] = value
    return out


def shallow(freqs):
    out = [None] * 8
    for rest in range(4):
        folded = four([freqs[4 * at + rest] for at in range(4)], -4)
        for at in range(4):
            value = turn(folded[at], -(at + 4) * rest)
            above = turn(value, -4 * rest)
            out[at] = value if rest == 0 else plus(out[at], value)
            out[at + 4] = above if rest == 0 else plus(out[at + 4], above)
    return out


def spectrum(in_ref, rows_ref):
    slabs, _, lanes = in_ref.shape
    high, low = pair_of(rows_ref, 0)
    length = high.shape[0] // 2
    parity = []
    for at in range(2):
        cells = in_ref[:, at * 8 : (at + 1) * 8, :].reshape(slabs * 8, lanes).T
        rows = slice(at * length, (at + 1) * length)
        parity.append(product(split(cells), (high[rows], low[rows]), NN))
    total_of, differ = parity[0] + parity[1], parity[0] - parity[1]
    real = jnp.concatenate([total_of[:, :length], differ[:, :length]], axis=1)
    imag = jnp.concatenate([total_of[:, length:], differ[:, length:]], axis=1)
    cols = lanes // 8
    return deepen([(real[at * cols : (at + 1) * cols], imag[at * cols : (at + 1) * cols]) for at in range(8)])


def at_depth(ref, at):
    cols = 16
    tiles = [
        ref[pl.ds(tile * 16 * cols + at, cols, stride=16), :] for tile in range(ref.shape[0] // (16 * cols))
    ]
    return jnp.concatenate(tiles, axis=1)


def total(values):
    return jnp.sum(jnp.sum(values, axis=0, keepdims=True), axis=1, keepdims=True)


def along(part, whole):
    return jnp.where(whole > 0.0, part / jnp.where(whole > 0.0, whole, 1.0), 0.0)


def row_of(value, lanes):
    return jnp.broadcast_to(value, (1, lanes))


def start_kernel(*refs):
    count = (len(refs) - 4) // 2
    sources, out_ref, loaded = refs[:count], refs[count], refs[count + 1 : 2 * count + 1]
    sems, *spaces = refs[2 * count + 1 :]
    vec_ref, sens_ref, table_ref = loaded[:3]
    half = table_ref.shape[0] // 2
    pairs = [(sources[at], loaded[at]) for at in range(2)]
    pairs += [(sources[2].at[pl.ds(at, half)], table_ref.at[pl.ds(at, half)]) for at in (0, half)]
    for source, target in zip(sources[3:], loaded[3:]):
        rows, lanes = source.shape[0], target.shape[1]
        for tile in range(source.shape[1] // lanes):
            pairs.append((source.at[:, pl.ds(tile * lanes, lanes)], target.at[pl.ds(tile * rows, rows)]))
    copies = [pltpu.make_async_copy(*pair, sems.at[at]) for at, pair in enumerate(pairs)]
    for copy in copies:
        copy.start()
    for copy in copies[:2]:
        copy.wait()
    cells = vec_ref.shape[0] // 2
    real, imag = coil_product(sens_ref, vec_ref[:cells], vec_ref[cells:])

    def table(part):
        copies[2 + part].wait()
        return table_ref[part * half : (part + 1) * half]

    send_columns(real, imag, table, out_ref, *spaces)
    for copy in copies[4:]:
        copy.wait()


def filter_kernel(in_ref, kernel_ref, rows_ref, out_ref, spec_ref):
    slabs, _, lanes = in_ref.shape
    spec = spectrum(in_ref, rows_ref)
    cols = lanes // 8
    filtered = []
    for at, (real, imag) in enumerate(spec):
        spec_ref[2 * at * cols : (2 * at + 1) * cols] = real
        spec_ref[(2 * at + 1) * cols : (2 * at + 2) * cols] = imag
        kernel = at_depth(kernel_ref, at)
        filtered.append((kernel * real, kernel * imag))
    planes = shallow(filtered)
    real, imag = [jnp.concatenate([plane[part] for plane in planes], axis=0) for part in range(2)]
    high, low = pair_of(rows_ref, 0)
    length = high.shape[0] // 2
    for at, join in enumerate((jnp.add, jnp.subtract)):
        folded = [join(part[:, :length], part[:, length:]) for part in (real, imag)]
        rows = slice(at * length, (at + 1) * length)
        back = product((high[rows], low[rows]), split(jnp.concatenate(folded, axis=1)), NT)
        out_ref[:, at * 8 : (at + 1) * 8, :] = back.reshape(slabs, 8, lanes)


def weigh_kernel(spec_ref, kernel_ref, vec_ref, _, norms_ref, by_depth_ref):
    cols = spec_ref.shape[0] // 32
    weight = 0.0
    for at in range(16):
        real, imag = spec_ref[2 * at * cols : (2 * at + 1) * cols], spec_ref[(2 * at + 1) * cols : (2 * at + 2) * cols]
        kernel = at_depth(kernel_ref, at)
        by_depth_ref[at * cols : (at + 1) * cols] = kernel
        weight = weight + kernel * (real * real + imag * imag)
    vec = vec_ref[...]
    lanes = norms_ref.shape[1]
    first = lax.broadcasted_iota(jnp.int32, norms_ref.shape, 0) == 0
    norms_ref[...] = jnp.where(first, row_of(total(weight), lanes), row_of(total(vec * vec), lanes))


def image_kernel(in_ref, sens_ref, table_ref, out_ref, straight_ref, turned_ref):
    slabs, _, lanes = in_ref.shape
    planes, blocks = 8, slabs // 8
    tiles = [
        jnp.concatenate(
            [
                in_ref[block * planes + at, part * 8 : (part + 1) * 8, :]
                for part in range(2)
                for block in range(blocks)
            ],
            axis=0,
        )
        for at in range(planes)
    ]
    tiles = exchange(tiles)
    spec = jnp.concatenate(
        [
            jnp.concatenate(
                [
                    tiles[plane][(part * blocks + block) * 8 : (part * blocks + block + 1) * 8]
                    for block in range(blocks)
                ],
                axis=1,
            )
            for part in range(2)
            for plane in range(planes)
        ],
        axis=0,
    )
    both = product(split(spec), pair_of(table_ref, 0), NT)
    by_real, by_imag = both[:, : both.shape[1] // 2], both[:, both.shape[1] // 2 :]
    cells = planes * 8
    tiled = range(by_real.shape[1] // 128)
    for parity in range(2):
        part = slice(parity * cells, (parity + 1) * cells)
        for tile in tiled:
            rows, tile_of = pl.ds(tile * 2 * cells + parity, cells, stride=2), slice(tile * 128, tile * 128 + 128)
            straight_ref[rows, :] = by_real[part, tile_of]
            turned_ref[rows, :] = by_imag[part, tile_of]

    def of_part(ref, part):
        columns = []
        for tile in tiled:
            starts = [tile * 2 * cells + 16 * plane + 8 * part for plane in range(planes)]
            columns.append(jnp.concatenate([ref[start : start + 8] for start in starts], axis=0))
        return jnp.concatenate(columns, axis=1)

    img_re = of_part(straight_ref, 0) + of_part(turned_ref, 1)
    img_im = of_part(straight_ref, 1) - of_part(turned_ref, 0)
    sens_re, sens_im = sens_ref[:cells], sens_ref[cells:]
    out_ref[:cells] = sens_re * img_re + sens_im * img_im
    out_ref[cells:] = sens_re * img_im - sens_im * img_re


def add_kernel(own_ref, across_ref, last_ref, next_ref, _, out_ref):
    out_ref[...] = (own_ref[...] + across_ref[...]) + (next_ref[...] + last_ref[...])


def turn_kernel(
    lam_ref, one_ref, other_ref, vec_ref, norms_ref, sens_ref, table_ref, out_ref, image_ref, sums_ref, straight_ref, turned_ref
):
    cells2, width = vec_ref.shape
    cells = cells2 // 2
    vec = vec_ref[...]
    image = (one_ref[...] + other_ref[...]) + lam_ref[0] * vec
    image_ref[...] = image
    real, imag = coil_product(sens_ref, image[:cells], image[cells:])
    send_columns(real, imag, pair_of(table_ref, 0).__getitem__, out_ref, straight_ref, turned_ref)
    norm = norms_ref[1:2, 0:1]
    ratio = along(total(vec * image), norm)
    rest = image - ratio * vec
    row = lax.broadcasted_iota(jnp.int32, sums_ref.shape, 0)
    lanes = sums_ref.shape[1]
    sums_ref[...] = jnp.where(
        row == 0,
        row_of(norm, lanes),
        jnp.where(row == 1, row_of(ratio, lanes), row_of(total(rest * rest), lanes)),
    )


def last_kernel(in_ref, before_ref, energy_ref, sums_ref, by_depth_ref, rows_ref, out_ref):
    spec = spectrum(in_ref, rows_ref)
    cols = spec[0][0].shape[0]
    norm = energy_ref[0:1, 0:1]

    def before(at):
        return before_ref[2 * at * cols : (2 * at + 1) * cols], before_ref[(2 * at + 1) * cols : (2 * at + 2) * cols]

    def kernel(at):
        return by_depth_ref[at * cols : (at + 1) * cols]

    weight = 0.0
    for at, (real, imag) in enumerate(spec):
        real_0, imag_0 = before(at)
        weight = weight + kernel(at) * (real * real_0 + imag * imag_0)
    ratio = along(total(weight), norm)
    weight = 0.0
    for at, (real, imag) in enumerate(spec):
        real_0, imag_0 = before(at)
        real, imag = real - ratio * real_0, imag - ratio * imag_0
        weight = weight + kernel(at) * (real * real + imag * imag)
    lanes = out_ref.shape[1]
    values = [
        row_of(norm, lanes),
        row_of(ratio, lanes),
        row_of(total(weight), lanes),
        sums_ref[0:1],
        sums_ref[1:2],
        sums_ref[2:3],
    ]
    lane = lax.broadcasted_iota(jnp.int32, (1, lanes), 1)
    line = values[-1]
    for at, value in enumerate(values[:-1]):
        line = jnp.where(lane == at, value, line)
    out_ref[...] = jnp.broadcast_to(line, out_ref.shape)


def solution_kernel(lam_ref, all_ref, vec_ref, image_ref, out_ref):
    lam = lam_ref[0]
    every = all_ref[...]
    lane = lax.broadcasted_iota(jnp.int32, every.shape, 1)

    def column(at):
        return jnp.sum(jnp.where(lane == at, every, 0.0), axis=1, keepdims=True)

    def sum_of(values):
        return jnp.sum(values, axis=0, keepdims=True)

    deep_norm, deep_ratio, deep_rest, norms, ratios, rests = [column(at) for at in range(6)]
    norm = sum_of(norms) * 0.125
    curvature = sum_of(ratios * norms) * 0.125
    step = norm / curvature
    left, deep_left = 1.0 - step * ratios, 1.0 - step * deep_ratio
    fresh = sum_of(left * left * norms + step * step * rests) * 0.125
    cross = sum_of(ratios * norms * left - step * rests) * 0.125
    energy_now = sum_of(deep_left * deep_left * deep_norm + step * step * deep_rest)
    ratio = fresh / norm
    bent = energy_now + lam * fresh + ratio * (2.0 * cross + ratio * curvature)
    step_now = along(fresh, bent)
    vec = vec_ref[...]
    residual = vec - step * image_ref[...]
    out_ref[...] = step * vec + step_now * (residual + ratio * vec)


def call(kernel, shapes, places, scratch=(), limit=16):
    spaces = {"s": pltpu.SMEM, "v": pltpu.VMEM, "h": pltpu.HBM}
    outs = [jax.ShapeDtypeStruct(shape, F32) if isinstance(shape, tuple) else shape for shape in shapes]
    out_specs = [pl.BlockSpec(memory_space=pltpu.VMEM)] * len(shapes)
    return pl.pallas_call(
        kernel,
        out_shape=outs if len(outs) > 1 else outs[0],
        in_specs=[pl.BlockSpec(memory_space=spaces[place]) for place in places],
        out_specs=out_specs if len(outs) > 1 else out_specs[0],
        scratch_shapes=list(scratch),
        compiler_params=pltpu.CompilerParams(vmem_limit_bytes=limit * 2**20),
    )


def shards(cotangent, sensitivity, kernel, reg_weight):
    planes, rows, width = cotangent.shape[1:]
    slabs = lax.axis_size("slab")
    coils = lax.axis_size("coil")
    cols = kernel.shape[0]
    cells2 = 2 * planes * rows
    vec = cotangent.reshape(cells2, width)
    sens = sensitivity.reshape(cells2, width)
    filt = kernel.reshape(cols * kernel.shape[1], kernel.shape[2])
    table = halves(plane_table(width), 0)
    row_table = halves(rows_table(width, slabs, 1.0 / math.sqrt(2 * planes)), 0)
    lanes = planes * cols
    block = (slabs, 2 * rows, lanes)
    to_slabs = partial(lax.all_to_all, axis_name="slab", split_axis=0, concat_axis=0, tiled=True)
    dma = pltpu.SemaphoreType.DMA

    spaces = [pltpu.VMEM((cells2 * width // 128, 128), F32)] * 2
    sources = [pltpu.with_memory_space_constraint(array, pltpu.HBM) for array in (vec, sens, table, filt, row_table)]
    loaded = [pltpu.VMEM(array.shape, array.dtype) for array in sources]
    loaded[3] = pltpu.VMEM((filt.size // 128, 128), F32)
    sent, vec, sens, table, filt, row_table = call(
        start_kernel, [block, *loaded], "hhhhh", [dma((len(sources) + filt.shape[1] // 128,)), *spaces]
    )(*sources)
    got = to_slabs(sent)
    back, before = call(filter_kernel, [block, (4 * lanes, 2 * width)], "vvv", (), 32)(got, filt, row_table)
    home = to_slabs(back)
    term = call(image_kernel, [(cells2, width)], "vvv", spaces)(home, sens, table)

    norms, filt = call(weigh_kernel, [(8, 128), (2 * lanes, 2 * width)], "vvvv")(before, filt, vec, term)

    chips = coils // 2

    def from_chip(shift):
        pairs = [
            (2 * chip + core, 2 * ((chip + shift) % chips) + core) for chip in range(chips) for core in range(2)
        ]
        return lax.ppermute(term, "coil", pairs)

    pair = call(add_kernel, [term.shape], "vvvvv")(term, *[from_chip(shift) for shift in (2, 3, 1)], norms)
    other = lax.ppermute(pair, "coil", [(at, at ^ 1) for at in range(coils)])
    sent, image, sums = call(turn_kernel, [block, (cells2, width), (8, 128)], "svvvvvv", spaces)(
        reg_weight, pair, other, vec, norms, sens, table
    )
    got = to_slabs(sent)
    own = call(last_kernel, [(coils * slabs, 128)], "vvvvvv", (), 32)(
        got, before, norms, sums, filt, row_table
    )
    every = lax.all_to_all(own, ("coil", "slab"), 0, 0, tiled=True)
    result = call(solution_kernel, [(cells2, width)], "svvv")(reg_weight, every, vec, image)
    return result.reshape(cotangent.shape)


def solution(mesh):
    in_specs = (
        P(None, None, "slab", None),
        P("coil", None, None, "slab", None),
        P("slab", None, None),
        P(),
    )
    out_specs = P(None, None, "slab", None)
    return jax.shard_map(shards, mesh=mesh, in_specs=in_specs, out_specs=out_specs, check_vma=False)
```

```python
from functools import partial
import math

import jax
import jax.numpy as jnp
import numpy as np
from jax import lax
from jax.experimental import pallas as pl
from jax.experimental.pallas import tpu as pltpu
from jax.sharding import PartitionSpec as P

F32 = jnp.float32
BF16 = jnp.bfloat16
NN = ((1,), (0,))
NT = ((1,), (1,))


def dft(length):
    grid_size = 2 * length
    winding = np.outer(np.arange(length) + length // 2, np.arange(grid_size)) % grid_size
    return np.exp(-2j * np.pi * winding / grid_size) / math.sqrt(grid_size)


def halves(table, axis):
    high = table.astype(np.float32).astype(jnp.bfloat16)
    low = (table - high.astype(np.float64)).astype(np.float32).astype(jnp.bfloat16)
    return jnp.asarray(np.concatenate([high, low], axis=axis))


def pair_of(ref, axis):
    half = ref.shape[axis] // 2
    return (ref[:half], ref[half:]) if axis == 0 else (ref[:, :half], ref[:, half:])


def plane_table(length):
    table = dft(length)
    return np.concatenate([table.real, table.imag], axis=0)


def rows_table(length, slabs, scale):
    pairs = length // slabs // 2
    table = scale * dft(length)[:, :length].reshape(slabs, pairs, 2, length).transpose(2, 0, 1, 3)
    out = np.empty((2, slabs, 2, pairs, 2, length))
    out[:, :, 0, :, 0], out[:, :, 1, :, 0] = table.real, -table.imag
    out[:, :, 0, :, 1], out[:, :, 1, :, 1] = table.imag, table.real
    return out.reshape(2 * length, 2 * length)


def split(values):
    high = values.astype(BF16)
    low = (values - high.astype(F32)).astype(BF16)
    return high, low


def product(left, right, dims):
    dot = partial(lax.dot_general, dimension_numbers=(dims, ((), ())), preferred_element_type=F32)
    rows, cols = left[0].shape[0], right[0].shape[1 - dims[1][0]]
    if dims == NT and cols <= 128:
        both = dot(left[0], jnp.concatenate(right, axis=0))
        return (both[:, :cols] + both[:, cols:]) + dot(left[1], right[0])
    both = dot(jnp.concatenate(left, axis=0), right[0])
    return (both[:rows] + both[rows:]) + dot(left[0], right[1])


def exchange(tiles):
    count = len(tiles)
    width = tiles[0].shape[1]
    step = width // count
    group = lax.broadcasted_iota(jnp.int32, tiles[0].shape, 1) // step
    tiles = [pltpu.roll(tile, step * at, 1) if at else tile for at, tile in enumerate(tiles)]
    half = 1
    while half < count:
        later = (group // half) % 2 == 1
        tiles = [jnp.where(later, tiles[(at + half) % count], tiles[at]) for at in range(count)]
        half *= 2
    return [pltpu.roll(tiles[-at], width - step * at, 1) if at else tiles[0] for at in range(count)]


def coil_product(sens_ref, real, imag):
    rows = real.shape[0]
    sens_re, sens_im = sens_ref[:rows], sens_ref[rows:]
    return sens_re * real - sens_im * imag, sens_re * imag + sens_im * real


def send_columns(real, imag, table, out_ref, straight_ref, turned_ref):
    cells, width = real.shape
    rows, grid_size = 8, 2 * width
    planes, blocks = cells // rows, grid_size // 128
    for plane in range(planes):
        for lanes in range(0, width, 128):
            at = 2 * rows * plane + lanes // 128 * 2 * cells
            one = real[rows * plane : rows * (plane + 1), lanes : lanes + 128]
            other = imag[rows * plane : rows * (plane + 1), lanes : lanes + 128]
            straight_ref[at : at + rows], straight_ref[at + rows : at + 2 * rows] = one, other
            turned_ref[at : at + rows], turned_ref[at + rows : at + 2 * rows] = -other, one

    tiled = range(0, width // 128 * 2 * cells, 2 * cells)
    parts = [
        jnp.concatenate(
            [ref[pl.ds(at + parity, cells, stride=2), :] for ref in (straight_ref, turned_ref) for at in tiled], axis=1
        )
        for parity in range(2)
    ]
    dot = partial(jnp.dot, preferred_element_type=F32)
    pair = split(jnp.concatenate(parts, axis=0))
    spec = dot(jnp.concatenate(pair, axis=0), table(0))
    spec = (spec[: 2 * cells] + spec[2 * cells :]) + dot(pair[0], table(1))
    tiles = [
        jnp.concatenate(
            [
                spec[(parity * planes + plane) * rows :][:rows, block * 128 : (block + 1) * 128]
                for parity in range(2)
                for block in range(blocks)
            ],
            axis=0,
        )
        for plane in range(planes)
    ]
    tiles = exchange(tiles)
    for parity in range(2):
        for block in range(blocks):
            for at in range(planes):
                start = (parity * blocks + block) * rows
                out_ref[block * planes + at, parity * rows : (parity + 1) * rows, :] = tiles[at][
                    start : start + rows
                ]


def turn(value, power):
    real, imag = value
    power %= 16
    if power == 0:
        return real, imag
    if power == 4:
        return imag, -real
    if power == 8:
        return -real, -imag
    if power == 12:
        return -imag, real
    cos, sin = math.cos(math.pi * power / 8), -math.sin(math.pi * power / 8)
    return cos * real - sin * imag, cos * imag + sin * real


def plus(one, other):
    return one[0] + other[0], one[1] + other[1]


def minus(one, other):
    return one[0] - other[0], one[1] - other[1]


def four(values, power):
    even, even_off = plus(values[0], values[2]), minus(values[0], values[2])
    odd, odd_off = plus(values[1], values[3]), turn(minus(values[1], values[3]), power)
    return plus(even, odd), plus(even_off, odd_off), minus(even, odd), minus(even_off, odd_off)


def deepen(cells):
    out = [None] * 16
    for rest in range(4):
        folded = [plus(cells[at], turn(cells[at + 4], 4 * rest)) for at in range(4)]
        folded = [turn(value, (at + 4) * rest) for at, value in enumerate(folded)]
        for at, value in enumerate(four(folded, 4)):
            out[4 * at + rest] = value
    return out


def shallow(freqs):
    out = [None] * 8
    for rest in range(4):
        folded = four([freqs[4 * at + rest] for at in range(4)], -4)
        for at in range(4):
            value = turn(folded[at], -(at + 4) * rest)
            above = turn(value, -4 * rest)
            out[at] = value if rest == 0 else plus(out[at], value)
            out[at + 4] = above if rest == 0 else plus(out[at + 4], above)
    return out


def spectrum(in_ref, rows_ref):
    slabs, _, lanes = in_ref.shape
    high, low = pair_of(rows_ref, 0)
    length = high.shape[0] // 2
    parity = []
    for at in range(2):
        cells = in_ref[:, at * 8 : (at + 1) * 8, :].reshape(slabs * 8, lanes).T
        rows = slice(at * length, (at + 1) * length)
        parity.append(product(split(cells), (high[rows], low[rows]), NN))
    total_of, differ = parity[0] + parity[1], parity[0] - parity[1]
    real = jnp.concatenate([total_of[:, :length], differ[:, :length]], axis=1)
    imag = jnp.concatenate([total_of[:, length:], differ[:, length:]], axis=1)
    cols = lanes // 8
    return deepen([(real[at * cols : (at + 1) * cols], imag[at * cols : (at + 1) * cols]) for at in range(8)])


def at_depth(ref, at):
    cols = 16
    tiles = [
        ref[pl.ds(tile * 16 * cols + at, cols, stride=16), :] for tile in range(ref.shape[0] // (16 * cols))
    ]
    return jnp.concatenate(tiles, axis=1)


def total(values):
    return jnp.sum(jnp.sum(values, axis=0, keepdims=True), axis=1, keepdims=True)


def along(part, whole):
    return jnp.where(whole > 0.0, part / jnp.where(whole > 0.0, whole, 1.0), 0.0)


def row_of(value, lanes):
    return jnp.broadcast_to(value, (1, lanes))


def start_kernel(*refs):
    count = (len(refs) - 4) // 2
    sources, out_ref, loaded = refs[:count], refs[count], refs[count + 1 : 2 * count + 1]
    sems, *spaces = refs[2 * count + 1 :]
    vec_ref, sens_ref, table_ref = loaded[:3]
    half = table_ref.shape[0] // 2
    pairs = [(sources[at], loaded[at]) for at in range(2)]
    pairs += [(sources[2].at[pl.ds(at, half)], table_ref.at[pl.ds(at, half)]) for at in (0, half)]
    for source, target in zip(sources[3:], loaded[3:]):
        rows, lanes = source.shape[0], target.shape[1]
        for tile in range(source.shape[1] // lanes):
            pairs.append((source.at[:, pl.ds(tile * lanes, lanes)], target.at[pl.ds(tile * rows, rows)]))
    copies = [pltpu.make_async_copy(*pair, sems.at[at]) for at, pair in enumerate(pairs)]
    for copy in copies:
        copy.start()
    for copy in copies[:2]:
        copy.wait()
    cells = vec_ref.shape[0] // 2
    real, imag = coil_product(sens_ref, vec_ref[:cells], vec_ref[cells:])

    def table(part):
        copies[2 + part].wait()
        return table_ref[part * half : (part + 1) * half]

    send_columns(real, imag, table, out_ref, *spaces)
    for copy in copies[4:]:
        copy.wait()


def filter_kernel(in_ref, kernel_ref, rows_ref, out_ref, spec_ref):
    slabs, _, lanes = in_ref.shape
    spec = spectrum(in_ref, rows_ref)
    cols = lanes // 8
    filtered = []
    for at, (real, imag) in enumerate(spec):
        spec_ref[2 * at * cols : (2 * at + 1) * cols] = real
        spec_ref[(2 * at + 1) * cols : (2 * at + 2) * cols] = imag
        kernel = at_depth(kernel_ref, at)
        filtered.append((kernel * real, kernel * imag))
    planes = shallow(filtered)
    real, imag = [jnp.concatenate([plane[part] for plane in planes], axis=0) for part in range(2)]
    high, low = pair_of(rows_ref, 0)
    length = high.shape[0] // 2
    for at, join in enumerate((jnp.add, jnp.subtract)):
        folded = [join(part[:, :length], part[:, length:]) for part in (real, imag)]
        rows = slice(at * length, (at + 1) * length)
        back = product((high[rows], low[rows]), split(jnp.concatenate(folded, axis=1)), NT)
        out_ref[:, at * 8 : (at + 1) * 8, :] = back.reshape(slabs, 8, lanes)


def weigh_kernel(spec_ref, kernel_ref, vec_ref, _, norms_ref, by_depth_ref, weighted_ref):
    cols = spec_ref.shape[0] // 32
    weight = 0.0
    for at in range(16):
        real, imag = spec_ref[2 * at * cols : (2 * at + 1) * cols], spec_ref[(2 * at + 1) * cols : (2 * at + 2) * cols]
        kernel = at_depth(kernel_ref, at)
        by_depth_ref[at * cols : (at + 1) * cols] = kernel
        heavy, heavy_imag = kernel * real, kernel * imag
        weighted_ref[2 * at * cols : (2 * at + 1) * cols] = heavy
        weighted_ref[(2 * at + 1) * cols : (2 * at + 2) * cols] = heavy_imag
        weight = weight + (heavy * real + heavy_imag * imag)
    vec = vec_ref[...]
    lanes = norms_ref.shape[1]
    first = lax.broadcasted_iota(jnp.int32, norms_ref.shape, 0) == 0
    norms_ref[...] = jnp.where(first, row_of(total(weight), lanes), row_of(total(vec * vec), lanes))


def image_kernel(in_ref, sens_ref, table_ref, out_ref, straight_ref, turned_ref):
    slabs, _, lanes = in_ref.shape
    planes, blocks = 8, slabs // 8
    tiles = [
        jnp.concatenate(
            [
                in_ref[block * planes + at, part * 8 : (part + 1) * 8, :]
                for part in range(2)
                for block in range(blocks)
            ],
            axis=0,
        )
        for at in range(planes)
    ]
    tiles = exchange(tiles)
    spec = jnp.concatenate(
        [
            jnp.concatenate(
                [
                    tiles[plane][(part * blocks + block) * 8 : (part * blocks + block + 1) * 8]
                    for block in range(blocks)
                ],
                axis=1,
            )
            for part in range(2)
            for plane in range(planes)
        ],
        axis=0,
    )
    both = product(split(spec), pair_of(table_ref, 0), NT)
    by_real, by_imag = both[:, : both.shape[1] // 2], both[:, both.shape[1] // 2 :]
    cells = planes * 8
    tiled = range(by_real.shape[1] // 128)
    for parity in range(2):
        part = slice(parity * cells, (parity + 1) * cells)
        for tile in tiled:
            rows, tile_of = pl.ds(tile * 2 * cells + parity, cells, stride=2), slice(tile * 128, tile * 128 + 128)
            straight_ref[rows, :] = by_real[part, tile_of]
            turned_ref[rows, :] = by_imag[part, tile_of]

    def of_part(ref, part):
        columns = []
        for tile in tiled:
            starts = [tile * 2 * cells + 16 * plane + 8 * part for plane in range(planes)]
            columns.append(jnp.concatenate([ref[start : start + 8] for start in starts], axis=0))
        return jnp.concatenate(columns, axis=1)

    img_re = of_part(straight_ref, 0) + of_part(turned_ref, 1)
    img_im = of_part(straight_ref, 1) - of_part(turned_ref, 0)
    sens_re, sens_im = sens_ref[:cells], sens_ref[cells:]
    out_ref[:cells] = sens_re * img_re + sens_im * img_im
    out_ref[cells:] = sens_re * img_im - sens_im * img_re


def add_kernel(own_ref, across_ref, last_ref, next_ref, _, out_ref):
    out_ref[...] = (own_ref[...] + across_ref[...]) + (next_ref[...] + last_ref[...])


def turn_kernel(
    lam_ref, one_ref, other_ref, vec_ref, norms_ref, sens_ref, table_ref, out_ref, image_ref, sums_ref, straight_ref, turned_ref
):
    cells2, width = vec_ref.shape
    cells = cells2 // 2
    vec = vec_ref[...]
    image = (one_ref[...] + other_ref[...]) + lam_ref[0] * vec
    image_ref[...] = image
    real, imag = coil_product(sens_ref, image[:cells], image[cells:])
    send_columns(real, imag, pair_of(table_ref, 0).__getitem__, out_ref, straight_ref, turned_ref)
    norm = norms_ref[1:2, 0:1]
    ratio = along(total(vec * image), norm)
    rest = image - ratio * vec
    row = lax.broadcasted_iota(jnp.int32, sums_ref.shape, 0)
    lanes = sums_ref.shape[1]
    sums_ref[...] = jnp.where(
        row == 0,
        row_of(norm, lanes),
        jnp.where(row == 1, row_of(ratio, lanes), row_of(total(rest * rest), lanes)),
    )


def last_kernel(in_ref, before_ref, weighted_ref, energy_ref, sums_ref, by_depth_ref, rows_ref, out_ref):
    spec = spectrum(in_ref, rows_ref)
    cols = spec[0][0].shape[0]
    norm = energy_ref[0:1, 0:1]

    def of(ref, at):
        return ref[2 * at * cols : (2 * at + 1) * cols], ref[(2 * at + 1) * cols : (2 * at + 2) * cols]

    def kernel(at):
        return by_depth_ref[at * cols : (at + 1) * cols]

    weight = 0.0
    for at, (real, imag) in enumerate(spec):
        real_0, imag_0 = of(weighted_ref, at)
        weight = weight + (real * real_0 + imag * imag_0)
    ratio = along(total(weight), norm)
    weight = 0.0
    for at, (real, imag) in enumerate(spec):
        real_0, imag_0 = of(before_ref, at)
        real, imag = real - ratio * real_0, imag - ratio * imag_0
        weight = weight + kernel(at) * (real * real + imag * imag)
    lanes = out_ref.shape[1]
    values = [
        row_of(norm, lanes),
        row_of(ratio, lanes),
        row_of(total(weight), lanes),
        sums_ref[0:1],
        sums_ref[1:2],
        sums_ref[2:3],
    ]
    lane = lax.broadcasted_iota(jnp.int32, (1, lanes), 1)
    line = values[-1]
    for at, value in enumerate(values[:-1]):
        line = jnp.where(lane == at, value, line)
    out_ref[...] = jnp.broadcast_to(line, out_ref.shape)


def solution_kernel(lam_ref, all_ref, vec_ref, image_ref, out_ref):
    lam = lam_ref[0]
    every = all_ref[...]
    lane = lax.broadcasted_iota(jnp.int32, every.shape, 1)

    def column(at):
        return jnp.sum(jnp.where(lane == at, every, 0.0), axis=1, keepdims=True)

    def sum_of(values):
        return jnp.sum(values, axis=0, keepdims=True)

    deep_norm, deep_ratio, deep_rest, norms, ratios, rests = [column(at) for at in range(6)]
    norm = sum_of(norms) * 0.125
    curvature = sum_of(ratios * norms) * 0.125
    step = norm / curvature
    left, deep_left = 1.0 - step * ratios, 1.0 - step * deep_ratio
    fresh = sum_of(left * left * norms + step * step * rests) * 0.125
    cross = sum_of(ratios * norms * left - step * rests) * 0.125
    energy_now = sum_of(deep_left * deep_left * deep_norm + step * step * deep_rest)
    ratio = fresh / norm
    bent = energy_now + lam * fresh + ratio * (2.0 * cross + ratio * curvature)
    step_now = along(fresh, bent)
    vec = vec_ref[...]
    residual = vec - step * image_ref[...]
    out_ref[...] = step * vec + step_now * (residual + ratio * vec)


def call(kernel, shapes, places, scratch=(), limit=16):
    spaces = {"s": pltpu.SMEM, "v": pltpu.VMEM, "h": pltpu.HBM}
    outs = [jax.ShapeDtypeStruct(shape, F32) if isinstance(shape, tuple) else shape for shape in shapes]
    out_specs = [pl.BlockSpec(memory_space=pltpu.VMEM)] * len(shapes)
    return pl.pallas_call(
        kernel,
        out_shape=outs if len(outs) > 1 else outs[0],
        in_specs=[pl.BlockSpec(memory_space=spaces[place]) for place in places],
        out_specs=out_specs if len(outs) > 1 else out_specs[0],
        scratch_shapes=list(scratch),
        compiler_params=pltpu.CompilerParams(vmem_limit_bytes=limit * 2**20),
    )


def shards(cotangent, sensitivity, kernel, reg_weight):
    planes, rows, width = cotangent.shape[1:]
    slabs = lax.axis_size("slab")
    coils = lax.axis_size("coil")
    cols = kernel.shape[0]
    cells2 = 2 * planes * rows
    vec = cotangent.reshape(cells2, width)
    sens = sensitivity.reshape(cells2, width)
    filt = kernel.reshape(cols * kernel.shape[1], kernel.shape[2])
    table = halves(plane_table(width), 0)
    row_table = halves(rows_table(width, slabs, 1.0 / math.sqrt(2 * planes)), 0)
    lanes = planes * cols
    block = (slabs, 2 * rows, lanes)
    to_slabs = partial(lax.all_to_all, axis_name="slab", split_axis=0, concat_axis=0, tiled=True)
    dma = pltpu.SemaphoreType.DMA

    spaces = [pltpu.VMEM((cells2 * width // 128, 128), F32)] * 2
    sources = [pltpu.with_memory_space_constraint(array, pltpu.HBM) for array in (vec, sens, table, filt, row_table)]
    loaded = [pltpu.VMEM(array.shape, array.dtype) for array in sources]
    loaded[3] = pltpu.VMEM((filt.size // 128, 128), F32)
    sent, vec, sens, table, filt, row_table = call(
        start_kernel, [block, *loaded], "hhhhh", [dma((len(sources) + filt.shape[1] // 128,)), *spaces]
    )(*sources)
    got = to_slabs(sent)
    back, before = call(filter_kernel, [block, (4 * lanes, 2 * width)], "vvv", (), 32)(got, filt, row_table)
    home = to_slabs(back)
    term = call(image_kernel, [(cells2, width)], "vvv", spaces)(home, sens, table)

    shapes = [(8, 128), (2 * lanes, 2 * width), (4 * lanes, 2 * width)]
    norms, filt, weighted = call(weigh_kernel, shapes, "vvvv")(before, filt, vec, term)

    chips = coils // 2

    def from_chip(shift):
        pairs = [
            (2 * chip + core, 2 * ((chip + shift) % chips) + core) for chip in range(chips) for core in range(2)
        ]
        return lax.ppermute(term, "coil", pairs)

    pair = call(add_kernel, [term.shape], "vvvvv")(term, *[from_chip(shift) for shift in (2, 3, 1)], norms)
    other = lax.ppermute(pair, "coil", [(at, at ^ 1) for at in range(coils)])
    sent, image, sums = call(turn_kernel, [block, (cells2, width), (8, 128)], "svvvvvv", spaces)(
        reg_weight, pair, other, vec, norms, sens, table
    )
    got = to_slabs(sent)
    own = call(last_kernel, [(coils * slabs, 128)], "vvvvvvv", (), 32)(
        got, before, weighted, norms, sums, filt, row_table
    )
    every = lax.all_to_all(own, ("coil", "slab"), 0, 0, tiled=True)
    result = call(solution_kernel, [(cells2, width)], "svvv")(reg_weight, every, vec, image)
    return result.reshape(cotangent.shape)


def solution(mesh):
    in_specs = (
        P(None, None, "slab", None),
        P("coil", None, None, "slab", None),
        P("slab", None, None),
        P(),
    )
    out_specs = P(None, None, "slab", None)
    return jax.shard_map(shards, mesh=mesh, in_specs=in_specs, out_specs=out_specs, check_vma=False)
```

```python
from functools import partial
import math

import jax
import jax.numpy as jnp
import numpy as np
from jax import lax
from jax.experimental import pallas as pl
from jax.experimental.pallas import tpu as pltpu
from jax.sharding import PartitionSpec as P

F32 = jnp.float32
BF16 = jnp.bfloat16
NN = ((1,), (0,))
NT = ((1,), (1,))


def dft(length):
    grid_size = 2 * length
    winding = np.outer(np.arange(length) + length // 2, np.arange(grid_size)) % grid_size
    return np.exp(-2j * np.pi * winding / grid_size) / math.sqrt(grid_size)


def halves(table, axis):
    high = table.astype(np.float32).astype(jnp.bfloat16)
    low = (table - high.astype(np.float64)).astype(np.float32).astype(jnp.bfloat16)
    return jnp.asarray(np.concatenate([high, low], axis=axis))


def pair_of(ref, axis):
    half = ref.shape[axis] // 2
    return (ref[:half], ref[half:]) if axis == 0 else (ref[:, :half], ref[:, half:])


def plane_table(length):
    table = dft(length)
    return np.concatenate([table.real, table.imag], axis=0)


def rows_table(length, slabs, scale):
    pairs = length // slabs // 2
    table = scale * dft(length)[:, :length].reshape(slabs, pairs, 2, length).transpose(2, 0, 1, 3)
    out = np.empty((2, slabs, 2, pairs, 2, length))
    out[:, :, 0, :, 0], out[:, :, 1, :, 0] = table.real, -table.imag
    out[:, :, 0, :, 1], out[:, :, 1, :, 1] = table.imag, table.real
    return out.reshape(2 * length, 2 * length)


def split(values):
    high = values.astype(BF16)
    low = (values - high.astype(F32)).astype(BF16)
    return high, low


def product(left, right, dims):
    dot = partial(lax.dot_general, dimension_numbers=(dims, ((), ())), preferred_element_type=F32)
    rows, cols = left[0].shape[0], right[0].shape[1 - dims[1][0]]
    if dims == NT and cols <= 128:
        both = dot(left[0], jnp.concatenate(right, axis=0))
        return (both[:, :cols] + both[:, cols:]) + dot(left[1], right[0])
    both = dot(jnp.concatenate(left, axis=0), right[0])
    return (both[:rows] + both[rows:]) + dot(left[0], right[1])


def exchange(tiles):
    count = len(tiles)
    width = tiles[0].shape[1]
    step = width // count
    group = lax.broadcasted_iota(jnp.int32, tiles[0].shape, 1) // step
    tiles = [pltpu.roll(tile, step * at, 1) if at else tile for at, tile in enumerate(tiles)]
    half = 1
    while half < count:
        later = (group // half) % 2 == 1
        tiles = [jnp.where(later, tiles[(at + half) % count], tiles[at]) for at in range(count)]
        half *= 2
    return [pltpu.roll(tiles[-at], width - step * at, 1) if at else tiles[0] for at in range(count)]


def coil_product(sens_ref, real, imag):
    rows = real.shape[0]
    sens_re, sens_im = sens_ref[:rows], sens_ref[rows:]
    return sens_re * real - sens_im * imag, sens_re * imag + sens_im * real


def send_columns(real, imag, table, out_ref, straight_ref, turned_ref):
    cells, width = real.shape
    rows, grid_size = 8, 2 * width
    planes, blocks = cells // rows, grid_size // 128
    for plane in range(planes):
        for lanes in range(0, width, 128):
            at = 2 * rows * plane + lanes // 128 * 2 * cells
            one = real[rows * plane : rows * (plane + 1), lanes : lanes + 128]
            other = imag[rows * plane : rows * (plane + 1), lanes : lanes + 128]
            straight_ref[at : at + rows], straight_ref[at + rows : at + 2 * rows] = one, other
            turned_ref[at : at + rows], turned_ref[at + rows : at + 2 * rows] = -other, one

    tiled = range(0, width // 128 * 2 * cells, 2 * cells)
    parts = [
        jnp.concatenate(
            [ref[pl.ds(at + parity, cells, stride=2), :] for ref in (straight_ref, turned_ref) for at in tiled], axis=1
        )
        for parity in range(2)
    ]
    dot = partial(jnp.dot, preferred_element_type=F32)
    pair = split(jnp.concatenate(parts, axis=0))
    spec = dot(jnp.concatenate(pair, axis=0), table(0))
    spec = (spec[: 2 * cells] + spec[2 * cells :]) + dot(pair[0], table(1))
    tiles = [
        jnp.concatenate(
            [
                spec[(parity * planes + plane) * rows :][:rows, block * 128 : (block + 1) * 128]
                for parity in range(2)
                for block in range(blocks)
            ],
            axis=0,
        )
        for plane in range(planes)
    ]
    tiles = exchange(tiles)
    for parity in range(2):
        for block in range(blocks):
            for at in range(planes):
                start = (parity * blocks + block) * rows
                out_ref[block * planes + at, parity * rows : (parity + 1) * rows, :] = tiles[at][
                    start : start + rows
                ]


def turn(value, power):
    real, imag = value
    power %= 16
    if power == 0:
        return real, imag
    if power == 4:
        return imag, -real
    if power == 8:
        return -real, -imag
    if power == 12:
        return -imag, real
    cos, sin = math.cos(math.pi * power / 8), -math.sin(math.pi * power / 8)
    return cos * real - sin * imag, cos * imag + sin * real


def plus(one, other):
    return one[0] + other[0], one[1] + other[1]


def minus(one, other):
    return one[0] - other[0], one[1] - other[1]


def four(values, power):
    even, even_off = plus(values[0], values[2]), minus(values[0], values[2])
    odd, odd_off = plus(values[1], values[3]), turn(minus(values[1], values[3]), power)
    return plus(even, odd), plus(even_off, odd_off), minus(even, odd), minus(even_off, odd_off)


def deepen(cells):
    out = [None] * 16
    for rest in range(4):
        folded = [plus(cells[at], turn(cells[at + 4], 4 * rest)) for at in range(4)]
        folded = [turn(value, (at + 4) * rest) for at, value in enumerate(folded)]
        for at, value in enumerate(four(folded, 4)):
            out[4 * at + rest] = value
    return out


def shallow(freqs):
    out = [None] * 8
    for rest in range(4):
        folded = four([freqs[4 * at + rest] for at in range(4)], -4)
        for at in range(4):
            value = turn(folded[at], -(at + 4) * rest)
            above = turn(value, -4 * rest)
            out[at] = value if rest == 0 else plus(out[at], value)
            out[at + 4] = above if rest == 0 else plus(out[at + 4], above)
    return out


def spectrum(in_ref, rows_ref):
    slabs, _, lanes = in_ref.shape
    high, low = pair_of(rows_ref, 0)
    length = high.shape[0] // 2
    parity = []
    for at in range(2):
        cells = in_ref[:, at * 8 : (at + 1) * 8, :].reshape(slabs * 8, lanes).T
        rows = slice(at * length, (at + 1) * length)
        parity.append(product(split(cells), (high[rows], low[rows]), NN))
    total_of, differ = parity[0] + parity[1], parity[0] - parity[1]
    real = jnp.concatenate([total_of[:, :length], differ[:, :length]], axis=1)
    imag = jnp.concatenate([total_of[:, length:], differ[:, length:]], axis=1)
    cols = lanes // 8
    return deepen([(real[at * cols : (at + 1) * cols], imag[at * cols : (at + 1) * cols]) for at in range(8)])


def at_depth(ref, at):
    cols = 16
    tiles = [
        ref[pl.ds(tile * 16 * cols + at, cols, stride=16), :] for tile in range(ref.shape[0] // (16 * cols))
    ]
    return jnp.concatenate(tiles, axis=1)


def total(values):
    return jnp.sum(jnp.sum(values, axis=0, keepdims=True), axis=1, keepdims=True)


def along(part, whole):
    return jnp.where(whole > 0.0, part / jnp.where(whole > 0.0, whole, 1.0), 0.0)


def row_of(value, lanes):
    return jnp.broadcast_to(value, (1, lanes))


def start_kernel(*refs):
    count = (len(refs) - 4) // 2
    sources, out_ref, loaded = refs[:count], refs[count], refs[count + 1 : 2 * count + 1]
    sems, *spaces = refs[2 * count + 1 :]
    vec_ref, sens_ref, table_ref = loaded[:3]
    half = table_ref.shape[0] // 2
    pairs = [(sources[at], loaded[at]) for at in range(2)]
    pairs += [(sources[2].at[pl.ds(at, half)], table_ref.at[pl.ds(at, half)]) for at in (0, half)]
    for source, target in zip(sources[3:], loaded[3:]):
        rows, lanes = source.shape[0], target.shape[1]
        for tile in range(source.shape[1] // lanes):
            pairs.append((source.at[:, pl.ds(tile * lanes, lanes)], target.at[pl.ds(tile * rows, rows)]))
    copies = [pltpu.make_async_copy(*pair, sems.at[at]) for at, pair in enumerate(pairs)]
    for copy in copies:
        copy.start()
    for copy in copies[:2]:
        copy.wait()
    cells = vec_ref.shape[0] // 2
    real, imag = coil_product(sens_ref, vec_ref[:cells], vec_ref[cells:])

    def table(part):
        copies[2 + part].wait()
        return table_ref[part * half : (part + 1) * half]

    send_columns(real, imag, table, out_ref, *spaces)
    for copy in copies[4:]:
        copy.wait()


def filter_kernel(in_ref, kernel_ref, rows_ref, out_ref, spec_ref):
    slabs, _, lanes = in_ref.shape
    spec = spectrum(in_ref, rows_ref)
    cols = lanes // 8
    filtered = []
    for at, (real, imag) in enumerate(spec):
        spec_ref[2 * at * cols : (2 * at + 1) * cols] = real
        spec_ref[(2 * at + 1) * cols : (2 * at + 2) * cols] = imag
        kernel = at_depth(kernel_ref, at)
        filtered.append((kernel * real, kernel * imag))
    planes = shallow(filtered)
    real, imag = [jnp.concatenate([plane[part] for plane in planes], axis=0) for part in range(2)]
    high, low = pair_of(rows_ref, 0)
    length = high.shape[0] // 2
    for at, join in enumerate((jnp.add, jnp.subtract)):
        folded = [join(part[:, :length], part[:, length:]) for part in (real, imag)]
        rows = slice(at * length, (at + 1) * length)
        back = product((high[rows], low[rows]), split(jnp.concatenate(folded, axis=1)), NT)
        out_ref[:, at * 8 : (at + 1) * 8, :] = back.reshape(slabs, 8, lanes)


def weigh_kernel(spec_ref, kernel_ref, vec_ref, _, norms_ref, by_depth_ref, weighted_ref):
    cols = spec_ref.shape[0] // 32
    weight = 0.0
    for at in range(16):
        real, imag = spec_ref[2 * at * cols : (2 * at + 1) * cols], spec_ref[(2 * at + 1) * cols : (2 * at + 2) * cols]
        kernel = at_depth(kernel_ref, at)
        by_depth_ref[at * cols : (at + 1) * cols] = kernel
        heavy, heavy_imag = kernel * real, kernel * imag
        weighted_ref[2 * at * cols : (2 * at + 1) * cols] = heavy
        weighted_ref[(2 * at + 1) * cols : (2 * at + 2) * cols] = heavy_imag
        weight = weight + (heavy * real + heavy_imag * imag)
    vec = vec_ref[...]
    lanes = norms_ref.shape[1]
    first = lax.broadcasted_iota(jnp.int32, norms_ref.shape, 0) == 0
    norms_ref[...] = jnp.where(first, row_of(total(weight), lanes), row_of(total(vec * vec), lanes))


def image_kernel(in_ref, sens_ref, table_ref, out_ref, straight_ref, turned_ref):
    slabs, _, lanes = in_ref.shape
    planes, blocks = 8, slabs // 8
    tiles = [
        jnp.concatenate(
            [
                in_ref[block * planes + at, part * 8 : (part + 1) * 8, :]
                for part in range(2)
                for block in range(blocks)
            ],
            axis=0,
        )
        for at in range(planes)
    ]
    tiles = exchange(tiles)
    spec = jnp.concatenate(
        [
            jnp.concatenate(
                [
                    tiles[plane][(part * blocks + block) * 8 : (part * blocks + block + 1) * 8]
                    for block in range(blocks)
                ],
                axis=1,
            )
            for part in range(2)
            for plane in range(planes)
        ],
        axis=0,
    )
    both = product(split(spec), pair_of(table_ref, 0), NT)
    by_real, by_imag = both[:, : both.shape[1] // 2], both[:, both.shape[1] // 2 :]
    cells = planes * 8
    tiled = range(by_real.shape[1] // 128)
    for parity in range(2):
        part = slice(parity * cells, (parity + 1) * cells)
        for tile in tiled:
            rows, tile_of = pl.ds(tile * 2 * cells + parity, cells, stride=2), slice(tile * 128, tile * 128 + 128)
            straight_ref[rows, :] = by_real[part, tile_of]
            turned_ref[rows, :] = by_imag[part, tile_of]

    def of_part(ref, part):
        columns = []
        for tile in tiled:
            starts = [tile * 2 * cells + 16 * plane + 8 * part for plane in range(planes)]
            columns.append(jnp.concatenate([ref[start : start + 8] for start in starts], axis=0))
        return jnp.concatenate(columns, axis=1)

    img_re = of_part(straight_ref, 0) + of_part(turned_ref, 1)
    img_im = of_part(straight_ref, 1) - of_part(turned_ref, 0)
    sens_re, sens_im = sens_ref[:cells], sens_ref[cells:]
    out_ref[:cells] = sens_re * img_re + sens_im * img_im
    out_ref[cells:] = sens_re * img_im - sens_im * img_re


def add_kernel(own_ref, across_ref, next_ref, last_ref, _, out_ref):
    out_ref[...] = (own_ref[...] + across_ref[...]) + (next_ref[...] + last_ref[...])


def turn_kernel(
    lam_ref, one_ref, other_ref, vec_ref, norms_ref, sens_ref, table_ref, out_ref, image_ref, sums_ref, straight_ref, turned_ref
):
    cells2, width = vec_ref.shape
    cells = cells2 // 2
    vec = vec_ref[...]
    image = (one_ref[...] + other_ref[...]) + lam_ref[0] * vec
    image_ref[...] = image
    real, imag = coil_product(sens_ref, image[:cells], image[cells:])
    send_columns(real, imag, pair_of(table_ref, 0).__getitem__, out_ref, straight_ref, turned_ref)
    norm = norms_ref[1:2, 0:1]
    ratio = along(total(vec * image), norm)
    rest = image - ratio * vec
    row = lax.broadcasted_iota(jnp.int32, sums_ref.shape, 0)
    lanes = sums_ref.shape[1]
    sums_ref[...] = jnp.where(
        row == 0,
        row_of(norm, lanes),
        jnp.where(row == 1, row_of(ratio, lanes), row_of(total(rest * rest), lanes)),
    )


def last_kernel(in_ref, before_ref, weighted_ref, energy_ref, sums_ref, by_depth_ref, rows_ref, out_ref):
    spec = spectrum(in_ref, rows_ref)
    cols = spec[0][0].shape[0]
    norm = energy_ref[0:1, 0:1]

    def of(ref, at):
        return ref[2 * at * cols : (2 * at + 1) * cols], ref[(2 * at + 1) * cols : (2 * at + 2) * cols]

    def kernel(at):
        return by_depth_ref[at * cols : (at + 1) * cols]

    weight = 0.0
    for at, (real, imag) in enumerate(spec):
        real_0, imag_0 = of(weighted_ref, at)
        weight = weight + (real * real_0 + imag * imag_0)
    ratio = along(total(weight), norm)
    weight = 0.0
    for at, (real, imag) in enumerate(spec):
        real_0, imag_0 = of(before_ref, at)
        real, imag = real - ratio * real_0, imag - ratio * imag_0
        weight = weight + kernel(at) * (real * real + imag * imag)
    lanes = out_ref.shape[1]
    values = [
        row_of(norm, lanes),
        row_of(ratio, lanes),
        row_of(total(weight), lanes),
        sums_ref[0:1],
        sums_ref[1:2],
        sums_ref[2:3],
    ]
    lane = lax.broadcasted_iota(jnp.int32, (1, lanes), 1)
    line = values[-1]
    for at, value in enumerate(values[:-1]):
        line = jnp.where(lane == at, value, line)
    out_ref[...] = jnp.broadcast_to(line, out_ref.shape)


def solution_kernel(lam_ref, all_ref, vec_ref, image_ref, out_ref):
    lam = lam_ref[0]
    every = all_ref[...]
    lane = lax.broadcasted_iota(jnp.int32, every.shape, 1)

    def column(at):
        return jnp.sum(jnp.where(lane == at, every, 0.0), axis=1, keepdims=True)

    def sum_of(values):
        return jnp.sum(values, axis=0, keepdims=True)

    deep_norm, deep_ratio, deep_rest, norms, ratios, rests = [column(at) for at in range(6)]
    norm = sum_of(norms) * 0.125
    curvature = sum_of(ratios * norms) * 0.125
    step = norm / curvature
    left, deep_left = 1.0 - step * ratios, 1.0 - step * deep_ratio
    fresh = sum_of(left * left * norms + step * step * rests) * 0.125
    cross = sum_of(ratios * norms * left - step * rests) * 0.125
    energy_now = sum_of(deep_left * deep_left * deep_norm + step * step * deep_rest)
    ratio = fresh / norm
    bent = energy_now + lam * fresh + ratio * (2.0 * cross + ratio * curvature)
    step_now = along(fresh, bent)
    vec = vec_ref[...]
    residual = vec - step * image_ref[...]
    out_ref[...] = step * vec + step_now * (residual + ratio * vec)


def call(kernel, shapes, places, scratch=(), limit=16):
    spaces = {"s": pltpu.SMEM, "v": pltpu.VMEM, "h": pltpu.HBM}
    outs = [jax.ShapeDtypeStruct(shape, F32) if isinstance(shape, tuple) else shape for shape in shapes]
    out_specs = [pl.BlockSpec(memory_space=pltpu.VMEM)] * len(shapes)
    return pl.pallas_call(
        kernel,
        out_shape=outs if len(outs) > 1 else outs[0],
        in_specs=[pl.BlockSpec(memory_space=spaces[place]) for place in places],
        out_specs=out_specs if len(outs) > 1 else out_specs[0],
        scratch_shapes=list(scratch),
        compiler_params=pltpu.CompilerParams(vmem_limit_bytes=limit * 2**20),
    )


def shards(cotangent, sensitivity, kernel, reg_weight):
    planes, rows, width = cotangent.shape[1:]
    slabs = lax.axis_size("slab")
    coils = lax.axis_size("coil")
    cols = kernel.shape[0]
    cells2 = 2 * planes * rows
    vec = cotangent.reshape(cells2, width)
    sens = sensitivity.reshape(cells2, width)
    filt = kernel.reshape(cols * kernel.shape[1], kernel.shape[2])
    table = halves(plane_table(width), 0)
    row_table = halves(rows_table(width, slabs, 1.0 / math.sqrt(2 * planes)), 0)
    lanes = planes * cols
    block = (slabs, 2 * rows, lanes)
    to_slabs = partial(lax.all_to_all, axis_name="slab", split_axis=0, concat_axis=0, tiled=True)
    dma = pltpu.SemaphoreType.DMA

    spaces = [pltpu.VMEM((cells2 * width // 128, 128), F32)] * 2
    sources = [pltpu.with_memory_space_constraint(array, pltpu.HBM) for array in (vec, sens, table, filt, row_table)]
    loaded = [pltpu.VMEM(array.shape, array.dtype) for array in sources]
    loaded[3] = pltpu.VMEM((filt.size // 128, 128), F32)
    sent, vec, sens, table, filt, row_table = call(
        start_kernel, [block, *loaded], "hhhhh", [dma((len(sources) + filt.shape[1] // 128,)), *spaces]
    )(*sources)
    got = to_slabs(sent)
    back, before = call(filter_kernel, [block, (4 * lanes, 2 * width)], "vvv", (), 32)(got, filt, row_table)
    home = to_slabs(back)
    term = call(image_kernel, [(cells2, width)], "vvv", spaces)(home, sens, table)

    shapes = [(8, 128), (2 * lanes, 2 * width), (4 * lanes, 2 * width)]
    norms, filt, weighted = call(weigh_kernel, shapes, "vvvv")(before, filt, vec, term)

    chips = coils // 2

    def from_chip(shift):
        pairs = [
            (2 * chip + core, 2 * ((chip + shift) % chips) + core) for chip in range(chips) for core in range(2)
        ]
        return lax.ppermute(term, "coil", pairs)

    pair = call(add_kernel, [term.shape], "vvvvv")(term, *[from_chip(shift) for shift in (2, 1, 3)], norms)
    other = lax.ppermute(pair, "coil", [(at, at ^ 1) for at in range(coils)])
    sent, image, sums = call(turn_kernel, [block, (cells2, width), (8, 128)], "svvvvvv", spaces)(
        reg_weight, pair, other, vec, norms, sens, table
    )
    got = to_slabs(sent)
    own = call(last_kernel, [(coils * slabs, 128)], "vvvvvvv", (), 32)(
        got, before, weighted, norms, sums, filt, row_table
    )
    every = lax.all_to_all(own, ("coil", "slab"), 0, 0, tiled=True)
    result = call(solution_kernel, [(cells2, width)], "svvv")(reg_weight, every, vec, image)
    return result.reshape(cotangent.shape)


def solution(mesh):
    in_specs = (
        P(None, None, "slab", None),
        P("coil", None, None, "slab", None),
        P("slab", None, None),
        P(),
    )
    out_specs = P(None, None, "slab", None)
    return jax.shard_map(shards, mesh=mesh, in_specs=in_specs, out_specs=out_specs, check_vma=False)
```
